256 devices in a mesh: fsdp: 32 (over z_lo, y, core), hst: 8 (over z_hi, x).
Axes of the slice: x: 4, y: 4, z: 8 (z_hi: 2, z_lo: 4; z = z_hi * 4 + z_lo), core: 2. Of those that a mesh axis runs over, the one named last changes fastest.
Arguments:
- tokens: bfloat16 [8192, 14848], P('fsdp'), may hold values from -6 to 6
- out_grad: bfloat16 [8192, 2048], P('fsdp', 'hst'), may hold values from -6 to 6
- param: float32 [14848, 2048], P('fsdp', 'hst'), may hold values from -0.125 to 0.125
- first: float32 [14848, 2048], P('fsdp', 'hst'), may hold values from -6 to 6
- second: float32 [14848, 2048], P('fsdp', 'hst'), may hold values from 0.25 to 4
- sources: int32 [8, 32, 8], P('hst'), may hold values from -1 to 511, as said below
Outputs:
- input_grad: bfloat16 [8192, 14848], P('fsdp', 'hst')
- new_state: float32 [3, 14848, 2048], P(None, 'fsdp', 'hst')
- backup_state: float32 [3, 14848, 2048], P(None, 'fsdp', 'hst')
- written: float32 [8, 32, 8, 29, 256], P('hst', 'fsdp')
The draws below stay inside these ranges and needn't reach their ends.
Inputs may be any that keep to these rules, and one draw needn't show every extreme that they name: `sources`: an entry s >= 0 names piece s % 16 of owner s // 16 in the host's own group; -1 is an empty slot and empty slots come after filled ones. Within one host no piece is named twice. A writer names at most 2 pieces of one owner, and some writer of every host names exactly 2; some writer of every host fills all 8 slots.
All inputs are finite; a program needn't handle non-finite values.
Results may differ from the reference program's by a relative error of at most 0.015.
Values may be sent and summed in bfloat16 or wider, within the bound.
A program may use at most 128 MiB of HBM per device.

```python
import math
import jax
import jax.numpy as jnp
from jax import lax

D = 14848
FF = 2048
TOK_DEV = 256
PIECES = 16
WCAP = 8
SCAP = 2
TOKENS = 8192
ROWS_P = 29
FW = 256
N_FSDP = 32
N_HST = 8


def draw_sources(key, part):
    key = jax.random.fold_in(key, 11)

    def one_host(host_key):
        key_order, key_levels, key_pieces = jax.random.split(host_key, 3)
        order = jax.random.permutation(key_order, N_FSDP)
        position = jnp.argsort(order)
        levels = jax.random.randint(key_levels, (N_FSDP,), 0, 4)
        loads = jnp.where(levels == 3, WCAP, levels + 1)
        loads = loads.at[0].set(WCAP)
        piece_order = jax.vmap(lambda k: jax.random.permutation(k, PIECES))(jax.random.split(key_pieces, N_FSDP))
        writer_pos = position[jnp.arange(N_FSDP)]
        slots = jnp.arange(WCAP)
        group = slots // SCAP
        owner = order[(writer_pos[:, None] + 1 + group[None, :]) % N_FSDP]
        piece = piece_order[owner, (group * SCAP + slots % SCAP)[None, :]]
        load = loads[writer_pos]
        return jnp.where(slots[None, :] < load[:, None], owner * PIECES + piece, -1).astype(jnp.int32)
    return jax.vmap(one_host)(jax.random.split(key, N_HST))


def spiked(result, own_key, source, target, shards_of, factor):
    owner, partner = [(jnp.arange(result.shape[dim]) // (result.shape[dim] // shards_of)).reshape([-1 if axis == dim else 1 for axis in range(result.ndim)]) for dim in (source, target)]
    chosen = jax.random.permutation(own_key, shards_of)[partner]
    strong = (owner == chosen) | (owner == (partner + shards_of // 2) % shards_of)
    return jnp.where(strong, factor * result, result)


def block_scale(own_key, shape, shards, low, largest):
    gain = 1.0
    for axis_at, parts in shards:
        heights = jax.random.uniform(jax.random.fold_in(jax.random.fold_in(own_key, 6), axis_at), (parts,), jnp.float32, low / len(shards), largest / len(shards))
        gain = gain * jnp.repeat(jnp.exp(heights), shape[axis_at] // parts).reshape((-1,) + (1,) * (len(shape) - 1 - axis_at))
    return gain


def bell_draw(rng, extent, deviation, bound, cuts=(), kind=jnp.bfloat16):
    array = jax.random.normal(rng, extent, jnp.float32) * deviation
    if len(cuts) > 0:
        array = block_scale(rng, extent, cuts, -0.22, 0.18) * array
    return jnp.clip(array, min=-bound, max=bound).astype(kind)


def bell_draw_with(rng, extent, width, reach, cuts, heavy, kind=jnp.bfloat16):
    values = width * jax.random.normal(rng, extent, jnp.float32)
    if cuts:
        values = values * block_scale(rng, extent, cuts, -0.22, 0.18)
    return jnp.clip(spiked(values, jax.random.fold_in(rng, 3), *heavy), -reach, reach).astype(kind)


def setup_inputs(seed: int = 0) -> dict:
    key_of = jax.random.split(jax.random.key(seed), 7)
    return {
        "tokens": bell_draw_with(key_of[0], (TOKENS, D), 1.0, 6.0, ((0, 32),), (0, 1, 32, 2.75)),
        "out_grad": bell_draw(key_of[1], (TOKENS, FF), 1.0, 6.0, ((0, 32), (1, 8))),
        "param": bell_draw(key_of[2], (D, FF), FF ** -0.5, 0.125, ((0, 32), (1, 8)), jnp.float32),
        "first": bell_draw(key_of[3], (D, FF), 1.0, 6.0, ((0, 32), (1, 8)), jnp.float32),
        "second": jnp.clip(jnp.exp(math.log(4.0) - 2.7725887 * jax.random.uniform(key_of[4], (D, FF), jnp.float32) ** block_scale(key_of[4], (D, FF), ((0, 32), (1, 8)), -0.2, 0.2)), 0.25, 4.0),
        "sources": draw_sources(jax.random.fold_in(key_of[6], 71), 0),
    }


def gelu_slope(pre):
    cdf = 0.5 * (1.0 + jax.scipy.special.erf(pre * 0.7071067811865476))
    pdf = jnp.exp(-0.5 * pre * pre) * 0.3989422804014327
    return cdf + pre * pdf

def adam_step(param, first, second, grad):
    moment = 0.8 * first + 0.2 * grad
    spread = 0.9 * second + 0.1 * grad * grad
    updated = param - 0.1 * (moment / (jnp.sqrt(spread) + 1e-08) + 0.1 * param)
    return (updated, moment, spread)

def reference(tokens, out_grad, param, first, second, sources):
    weight16 = param.astype(jnp.bfloat16)
    pre = jnp.dot(tokens, weight16, preferred_element_type=jnp.float32)
    dz = (out_grad.astype(jnp.float32) * gelu_slope(pre)).astype(jnp.bfloat16)
    token_blocks = tokens.reshape(N_FSDP, TOK_DEV, D)
    dz_blocks = dz.reshape(N_FSDP, TOK_DEV, FF)

    def add_block(total, pair):
        part = jnp.dot(pair[0].T, pair[1], preferred_element_type=jnp.float32)
        return (total + lax.optimization_barrier(part.astype(jnp.bfloat16)).astype(jnp.float32), None)
    grad_sum, _ = lax.scan(add_block, jnp.zeros((D, FF), jnp.float32), (token_blocks, dz_blocks))
    grad = grad_sum / jnp.sqrt(jnp.float32(TOKENS))
    dz_hosts = dz.reshape(TOKENS, N_HST, FW).transpose(1, 0, 2)
    weight_hosts = weight16.reshape(D, N_HST, FW).transpose(1, 0, 2)

    def add_host(total, pair):
        part = jnp.dot(pair[0], pair[1].T, preferred_element_type=jnp.float32)
        return (total + lax.optimization_barrier(part.astype(jnp.bfloat16)).astype(jnp.float32), None)
    input_sum, _ = lax.scan(add_host, jnp.zeros((TOKENS, D), jnp.float32), (dz_hosts, weight_hosts))
    input_grad = input_sum.astype(jnp.bfloat16)
    updated, moment, spread = adam_step(param, first, second, grad)
    new_state = jnp.stack([updated, moment, spread])
    backup_state = jnp.roll(new_state.reshape(3, D, N_HST, FW), 1, axis=2).reshape(3, D, FF)
    table = updated.reshape(N_FSDP, PIECES, ROWS_P, N_HST, FW).transpose(3, 0, 1, 2, 4)
    table = table.reshape(N_HST, N_FSDP * PIECES, ROWS_P, FW)

    def pick_host(tab, src):
        picked = jnp.take(tab, jnp.maximum(src, 0).reshape(-1), axis=0)
        picked = picked.reshape(N_FSDP, WCAP, ROWS_P, FW)
        return jnp.where((src >= 0)[:, :, None, None], picked, jnp.float32(0.0))
    written = jax.vmap(pick_host)(table, sources)
    return (input_grad, new_state, backup_state, written)
```

```python
import functools

import jax
import jax.numpy as jnp
from jax import lax
from jax.experimental import pallas as pl
from jax.experimental.pallas import tpu as pltpu
from jax.sharding import PartitionSpec as P

PIECES = 16
WCAP = 8
SCAP = 2
MESH = pl.DeviceIdType.MESH
BF16 = jnp.bfloat16
F32 = jnp.float32
NZ, NY = 4, 4
TOK = 256
RB = 464
CB = 256
HA = 240


def gelu_slope(pre):
    cdf = 0.5 * (1.0 + lax.erf(pre * 0.7071067811865476))
    pdf = jnp.exp(-0.5 * pre * pre) * 0.3989422804014327
    return cdf + pre * pdf


def adam_step(param, first, second, grad):
    moment = 0.8 * first + 0.2 * grad
    spread = 0.9 * second + 0.1 * grad * grad
    updated = param - 0.1 * (moment / (jnp.sqrt(spread) + 1e-08) + 0.1 * param)
    return (updated, moment, spread)


def rows_of(f):
    return pl.ds(pl.multiple_of(f * RB, 16), RB)


def core_kernel(
    tokens, out_grad, param, grad_out, dz_out,
    tok, tokT, w, part, rxp, chip, sendh, rxh, sendf, rxf, sendz, rxz,
    tok_sem, ag_s, ag_r, rs_s, rs_r,
):
    f = lax.axis_index("fsdp")
    z, y, c = f // 8, (f // 2) % 4, f % 2
    yr, yl, yo = (y + 1) % 4, (y + 3) % 4, (y + 2) % 4
    zk = [z, z + 1 - 2 * (z % 2), (z + 2) % 4, 3 - z]

    def at(zz, yy, cc):
        return {"fsdp": zz * 8 + yy * 2 + cc}

    def idx(zz, yy, cc):
        return zz * 8 + yy * 2 + cc

    right, left, partner = at(z, yr, c), at(z, yl, c), at(z, y, 1 - c)

    tok_copy = pltpu.make_async_copy(tokens, tok, tok_sem)
    tok_copy.start()
    w[rows_of(f), :] = param[...].astype(BF16)

    barrier = pltpu.get_barrier_semaphore()
    for peer in (right, left, partner, at(zk[1], y, c), at(zk[2], y, c), at(zk[3], y, c)):
        pl.semaphore_signal(barrier, inc=1, device_id=peer, device_id_type=MESH)
    pl.semaphore_wait(barrier, 6)

    pending = []

    def send(src, dst, s_sem, r_sem, to):
        copy = pltpu.make_async_remote_copy(
            src_ref=src, dst_ref=dst, send_sem=s_sem, recv_sem=r_sem, device_id=to, device_id_type=MESH
        )
        copy.start()
        pending.append(copy)
        return copy

    def ag_send(block, lo, n, k, j, to):
        ref = w.at[pl.ds(pl.multiple_of(block * RB + lo, 16), n), :]
        return send(ref, ref, ag_s.at[k * 8 + j], ag_r.at[k * 8 + j], to)

    zsend = {}
    own = [None] * 4
    core = {}

    def issue(k):
        b = idx(zk[k], y, c)
        own[k] = (ag_send(b, 0, RB, k, 0, right), ag_send(b, 0, RB, k, 1, left))
        core[k, 0] = ag_send(b, 0, RB, k, 4, partner)

    issue(0)
    for k in (1, 2, 3):
        ref = w.at[rows_of(f), :]
        zsend[k] = send(ref, ref, ag_s.at[32 + k], ag_r.at[32 + k], at(zk[k], y, c))

    tok_copy.wait()

    def transpose_some(lo, hi):
        def step(i, carry):
            cols = pl.ds(pl.multiple_of(i * 512, 512), 512)
            tokT[cols, :] = tok[:, cols].T
            return carry

        lax.fori_loop(lo, hi, step, 0)

    halves = {}

    def forward(k):
        own[k][0].wait_recv()
        b = idx(zk[k], yl, c)
        ha = ag_send(b, 0, HA, k, 2, right)
        core[k, 1] = ag_send(b, 0, RB, k, 5, partner)
        own[k][1].wait_recv()
        b = idx(zk[k], yr, c)
        hb = ag_send(b, HA, RB - HA, k, 3, left)
        core[k, 2] = ag_send(b, 0, RB, k, 6, partner)
        halves[k] = (ha, hb)

    def last(k):
        halves[k][0].wait_recv()
        halves[k][1].wait_recv()
        core[k, 3] = ag_send(idx(zk[k], yo, c), 0, RB, k, 7, partner)

    transpose_some(0, 8)
    zsend[1].wait_recv()
    issue(1)
    forward(0)
    transpose_some(8, 15)
    zsend[2].wait_recv()
    issue(2)
    last(0)
    forward(1)
    transpose_some(15, 22)
    zsend[3].wait_recv()
    issue(3)
    last(1)
    forward(2)
    transpose_some(22, 29)
    last(2)
    forward(3)
    last(3)
    for k in range(4):
        for j in range(4):
            core[k, j].wait_recv()

    def pre_step(i, acc):
        cols = pl.ds(pl.multiple_of(i * 3712, 128), 3712)
        return acc + jnp.dot(tok[:, cols], w[cols, :], preferred_element_type=F32)

    pre = lax.fori_loop(0, 4, pre_step, jnp.zeros((TOK, CB), F32))
    dz = (out_grad[...].astype(F32) * gelu_slope(pre)).astype(BF16)
    dz_out[...] = dz

    swap = []
    for s, k in enumerate((3, 2, 1, 0)):
        def partner_block(j, carry, k=k, s=s):
            part[s, j] = jnp.dot(
                tokT[rows_of(idx(zk[k], j, 1 - c)), :], dz_out[...], preferred_element_type=F32
            ).astype(BF16)
            return carry

        lax.fori_loop(0, 4, partner_block, 0)
        swap.append(send(part.at[s], rxp.at[s], rs_s.at[s], rs_r.at[s], partner))

    def chip_block(k, s, yy):
        mine = jnp.dot(tokT[rows_of(idx(zk[k], yy, c)), :], dz_out[...], preferred_element_type=F32)
        return mine + rxp[s, yy].astype(F32)

    hsend = []
    for s, k in enumerate((3, 2, 1, 0)):
        swap[s].wait_recv()
        sendh[s] = chip_block(k, s, yo).astype(BF16)
        a = send(sendh.at[s, pl.ds(0, HA)], rxh.at[s, pl.ds(0, HA)], rs_s.at[4 + s], rs_r.at[4 + s], right)
        b = send(
            sendh.at[s, pl.ds(HA, RB - HA)], rxh.at[s, pl.ds(HA, RB - HA)], rs_s.at[8 + s], rs_r.at[8 + s], left
        )
        hsend.append((a, b))
        chip[s, 0] = chip_block(k, s, yr)
        chip[s, 1] = chip_block(k, s, yl)
        chip[s, 2] = chip_block(k, s, y)

    fsend = []
    zout = []

    def full(s):
        hsend[s][0].wait_recv()
        sendf[s, 0, pl.ds(0, HA)] = (chip[s, 0, pl.ds(0, HA)] + rxh[s, pl.ds(0, HA)].astype(F32)).astype(BF16)
        sendf[s, 0, pl.ds(HA, RB - HA)] = chip[s, 0, pl.ds(HA, RB - HA)].astype(BF16)
        a = send(sendf.at[s, 0], rxf.at[s, 0], rs_s.at[12 + s], rs_r.at[12 + s], right)
        hsend[s][1].wait_recv()
        sendf[s, 1, pl.ds(0, HA)] = chip[s, 1, pl.ds(0, HA)].astype(BF16)
        sendf[s, 1, pl.ds(HA, RB - HA)] = (
            chip[s, 1, pl.ds(HA, RB - HA)] + rxh[s, pl.ds(HA, RB - HA)].astype(F32)
        ).astype(BF16)
        b = send(sendf.at[s, 1], rxf.at[s, 1], rs_s.at[16 + s], rs_r.at[16 + s], left)
        fsend.append((a, b))

    def ring_sum(s):
        fsend[s][0].wait_recv()
        fsend[s][1].wait_recv()
        return chip[s, 2] + rxf[s, 0].astype(F32) + rxf[s, 1].astype(F32)

    def line(s, k):
        sendz[s] = ring_sum(s).astype(BF16)
        zout.append(send(sendz.at[s], rxz.at[s], rs_s.at[20 + s], rs_r.at[20 + s], at(zk[k], y, c)))

    full(0)
    full(1)
    line(0, 3)
    full(2)
    line(1, 2)
    full(3)
    line(2, 1)
    total = ring_sum(3)
    for s in range(3):
        zout[s].wait_recv()
        total = total + rxz[s].astype(F32)
    grad_out[...] = total * (1.0 / 90.50966799187809)
    for copy in pending:
        copy.wait_send()


def core_call(tokens, out_grad, param):
    vmem = pl.BlockSpec(memory_space=pltpu.VMEM)
    return pl.pallas_call(
        core_kernel,
        name="slab",
        out_shape=(jax.ShapeDtypeStruct((RB, CB), F32), jax.ShapeDtypeStruct((TOK, CB), BF16)),
        in_specs=[pl.BlockSpec(memory_space=pl.ANY), vmem, vmem],
        out_specs=(vmem, vmem),
        scratch_shapes=[
            pltpu.VMEM((TOK, 32 * RB), BF16),
            pltpu.VMEM((32 * RB, TOK), BF16),
            pltpu.VMEM((32 * RB, CB), BF16),
            pltpu.VMEM((4, 4, RB, CB), BF16),
            pltpu.VMEM((4, 4, RB, CB), BF16),
            pltpu.VMEM((4, 3, RB, CB), F32),
            pltpu.VMEM((4, RB, CB), BF16),
            pltpu.VMEM((4, RB, CB), BF16),
            pltpu.VMEM((4, 2, RB, CB), BF16),
            pltpu.VMEM((4, 2, RB, CB), BF16),
            pltpu.VMEM((3, RB, CB), BF16),
            pltpu.VMEM((3, RB, CB), BF16),
            pltpu.SemaphoreType.DMA,
            pltpu.SemaphoreType.DMA((36,)),
            pltpu.SemaphoreType.DMA((36,)),
            pltpu.SemaphoreType.DMA((24,)),
            pltpu.SemaphoreType.DMA((24,)),
        ],
        compiler_params=pltpu.CompilerParams(
            collective_id=0, has_side_effects=True, vmem_limit_bytes=60 * 1024 * 1024
        ),
        cost_estimate=pl.CostEstimate(flops=4 * TOK * 32 * RB * CB, bytes_accessed=300_000_000, transcendentals=TOK * CB),
    )(tokens, out_grad, param)


def from_behind(value, axis, steps):
    count = lax.axis_size(axis)
    pairs = [(source, (source + steps) % count) for source in range(count)]
    return lax.ppermute(value, axis, pairs)


def on_device(tokens, out_grad, param, first, second, sources):
    row_count = param.shape[0]
    col_count = param.shape[1]
    weight16 = param.astype(BF16)
    pairs = [(f * 8 + h, (4 * h + f % 4) * 8 + f // 4) for f in range(32) for h in range(8)]
    w2 = lax.all_gather(lax.ppermute(weight16, ("fsdp", "hst"), pairs), "fsdp", axis=0)
    grad, dz = core_call(tokens, out_grad, param)
    dz_all = lax.all_gather(dz, "hst", axis=0)
    w2 = w2.reshape(8, 4 * RB, CB)
    input_grad = lax.dot_general(
        dz_all.transpose(1, 0, 2).reshape(TOK, 8 * CB),
        w2.transpose(1, 0, 2).reshape(4 * RB, 8 * CB),
        (((1,), (1,)), ((), ())),
        preferred_element_type=F32,
    ).astype(BF16)
    updated, moment, spread = adam_step(param, first, second, grad)
    new_state = jnp.stack([updated, moment, spread])
    backup_state = from_behind(new_state.astype(BF16), "hst", 1).astype(new_state.dtype)
    me = lax.axis_index("fsdp")
    fsdp_count = lax.axis_size("fsdp")
    table = sources[0]
    rows_piece = row_count // PIECES
    owners = table // PIECES
    mine = (owners == me) & (table >= 0)
    rank = jnp.cumsum(mine.astype(jnp.int32), axis=1) - 1
    slot_pick = mine[:, None, :] & (
        rank[:, None, :] == jnp.arange(SCAP, dtype=jnp.int32)[None, :, None]
    )
    piece_of = table % PIECES
    piece_match = (
        piece_of[:, None, :, None] == jnp.arange(PIECES, dtype=jnp.int32)[None, None, None, :]
    )
    selector = jnp.sum((slot_pick[..., None] & piece_match).astype(jnp.float32), axis=2)
    flat_pieces = updated.reshape(PIECES, rows_piece * col_count)
    outgoing = jnp.einsum("dkp,pq->dkq", selector, flat_pieces, precision=lax.Precision.HIGHEST)
    arrived = lax.all_to_all(
        outgoing.astype(jnp.bfloat16), "fsdp", split_axis=0, concat_axis=0, tiled=True
    ).astype(outgoing.dtype)
    own_row = lax.dynamic_index_in_dim(table, me, 0, keepdims=False)
    own_owner = own_row // PIECES
    valid = own_row >= 0
    slot_ids = jnp.arange(WCAP, dtype=jnp.int32)
    earlier = (slot_ids[None, :] < slot_ids[:, None]) & (own_owner[None, :] == own_owner[:, None])
    own_rank = jnp.sum(earlier.astype(jnp.int32), axis=1)
    index = jnp.maximum(own_owner, 0) * SCAP + own_rank
    picked = jnp.take(arrived.reshape(fsdp_count * SCAP, rows_piece * col_count), index, axis=0)
    picked = jnp.where(valid[:, None], picked, jnp.float32(0.0))
    written = picked.reshape(1, 1, WCAP, rows_piece, col_count)
    return (input_grad, new_state, backup_state, written)


def solution(mesh):
    return jax.shard_map(
        on_device,
        mesh=mesh,
        in_specs=(
            P("fsdp", None),
            P("fsdp", "hst"),
            P("fsdp", "hst"),
            P("fsdp", "hst"),
            P("fsdp", "hst"),
            P("hst", None, None),
        ),
        out_specs=(
            P("fsdp", "hst"),
            P(None, "fsdp", "hst"),
            P(None, "fsdp", "hst"),
            P("hst", "fsdp", None, None, None),
        ),
        check_vma=False,
    )
```

```python
import functools

import jax
import jax.numpy as jnp
from jax import lax
from jax.experimental import pallas as pl
from jax.experimental.pallas import tpu as pltpu
from jax.sharding import PartitionSpec as P

MESH = pl.DeviceIdType.MESH
BF16 = jnp.bfloat16
F32 = jnp.float32
I32 = jnp.int32
TOK = 256
RB = 464
CB = 256
DM = 32 * RB
IG = DM // 8
HA = 240
PC = 29
PR = 64
SR = 32
QS, QR = 112, 128


def gelu_slope(pre):
    cdf = 0.5 * (1.0 + lax.erf(pre * 0.7071067811865476))
    pdf = jnp.exp(-0.5 * pre * pre) * 0.3989422804014327
    return cdf + pre * pdf


def adam_step(param, first, second, grad):
    moment = 0.8 * first + 0.2 * grad
    spread = 0.9 * second + 0.1 * grad * grad
    updated = param - 0.1 * (moment / (jnp.sqrt(spread) + 1e-08) + 0.1 * param)
    return (updated, moment, spread)


def rows_of(f):
    return pl.ds(pl.multiple_of(f * RB, 16), RB)


def dot_t(a, b):
    return lax.dot_general(a, b, (((1,), (1,)), ((), ())), preferred_element_type=F32)


def kernel(
    tokens, out_grad, param, first_in, second_in, sources,
    input_grad, new_state, backup, written,
    tok, tokT, w, w2, rxp, sendh, rxh, sendf, rxf, sendz, rxz, dz_own, dz_all,
    first, second, st, nst, st1, st2, gp, ngp, gp1, gp2, acc, grad, p16,
    pick, merge, offer, taken, taken2, merged, rxm,
    in_sem, ag_s, ag_r, bg_s, bg_r, rs_s, rs_r, dz_s, dz_r, pe_s, pe_r, re_s, re_r, wr_s, wr_r,
):
    f = lax.axis_index("fsdp")
    h = lax.axis_index("hst")
    z, y, c = f // 8, (f // 2) % 4, f % 2
    hi, x = h // 4, h % 4
    yr, yl, yo = (y + 1) % 4, (y + 3) % 4, (y + 2) % 4
    zk = [z, z + 1 - 2 * (z % 2), (z + 2) % 4, 3 - z]

    def idx(zz, yy, cc):
        return zz * 8 + yy * 2 + cc

    def at(zz, yy, cc):
        return {"fsdp": idx(zz, yy, cc)}

    def over(ww, xx):
        return {"hst": ww * 4 + xx}

    right, left, partner, across = at(z, yr, c), at(z, yl, c), at(z, y, 1 - c), at(z, yo, c)
    line_to = [None] + [at(zk[k], y, c) for k in (1, 2, 3)]
    opposite = over(1 - hi, x)
    xs = [over(hi, (x + i) % 4) for i in (1, 2, 3)]
    swapped = {"fsdp": 4 * h + f % 4, "hst": f // 4}
    moves = f // 4 != h

    loads = [
        pltpu.make_async_copy(a, b, in_sem.at[i])
        for i, (a, b) in enumerate(((tokens, tok), (first_in, first), (second_in, second)))
    ]
    for load in loads:
        load.start()
    w[rows_of(f), :] = param[...].astype(BF16)

    barrier = pltpu.get_barrier_semaphore()
    for peer in (right, left, across, partner, *line_to[1:], opposite, *xs):
        pl.semaphore_signal(barrier, inc=1, device_id=peer, device_id_type=MESH)

    @pl.when(moves)
    def _():
        pl.semaphore_signal(barrier, inc=1, device_id=swapped, device_id_type=MESH)
        pl.semaphore_wait(barrier, 12)

    @pl.when(jnp.logical_not(moves))
    def _():
        pl.semaphore_wait(barrier, 11)

    pending = []

    def remote(src, dst, s_sem, r_sem, to):
        return pltpu.make_async_remote_copy(
            src_ref=src, dst_ref=dst, send_sem=s_sem, recv_sem=r_sem, device_id=to, device_id_type=MESH
        )

    def send(src, dst, s_sem, r_sem, to):
        copy = remote(src, dst, s_sem, r_sem, to)
        copy.start()
        pending.append(copy)
        return copy

    class Gather:
        def __init__(self, buf, s_sem, r_sem):
            self.buf, self.s, self.r = buf, s_sem, r_sem
            self.own, self.core, self.halves, self.zs, self.sent = {}, {}, {}, {}, []

        def put(self, block, lo, n, sem, to):
            ref = self.buf.at[pl.ds(pl.multiple_of(block * RB + lo, 16), n), :]
            copy = remote(ref, ref, self.s.at[sem], self.r.at[sem], to)
            copy.start()
            self.sent.append(copy)
            return copy

        def lines(self):
            for k in (1, 2, 3):
                self.zs[k] = self.put(f, 0, RB, 32 + k, line_to[k])

        def issue(self, k):
            if k:
                self.zs[k].wait_recv()
            b = idx(zk[k], y, c)
            self.own[k] = (self.put(b, 0, RB, k * 8, right), self.put(b, 0, RB, k * 8 + 1, left))
            self.core[k, 0] = self.put(b, 0, RB, k * 8 + 4, partner)

        def forward(self, k):
            self.own[k][0].wait_recv()
            b = idx(zk[k], yl, c)
            one = self.put(b, 0, HA, k * 8 + 2, right)
            self.core[k, 1] = self.put(b, 0, RB, k * 8 + 5, partner)
            self.own[k][1].wait_recv()
            b = idx(zk[k], yr, c)
            two = self.put(b, HA, RB - HA, k * 8 + 3, left)
            self.core[k, 2] = self.put(b, 0, RB, k * 8 + 6, partner)
            self.halves[k] = (one, two)

        def last(self, k):
            self.halves[k][0].wait_recv()
            self.halves[k][1].wait_recv()
            self.core[k, 3] = self.put(idx(zk[k], yo, c), 0, RB, k * 8 + 7, partner)

        def wait_core(self, k):
            for j in range(4):
                self.core[k, j].wait_recv()

    def transpose_some(lo, hi_):
        def step(i, carry):
            cols = pl.ds(pl.multiple_of(i * 512, 512), 512)
            tokT[cols, :] = tok[:, cols].T
            return carry

        lax.fori_loop(lo, hi_, step, 0)

    class Relay:
        def __init__(self, src, dst, one, two, sem):
            self.src, self.dst, self.one, self.two = src, dst, one, two
            self.s = [re_s.at[sem + i] for i in range(7)]
            self.r = [re_r.at[sem + i] for i in range(7)]

        def to_next(self):
            return remote(self.src, self.dst, self.s[0], self.r[0], over(hi, (x + 1) % 4))

        def to_column(self, q):
            return remote(self.src.at[q], self.one, self.s[1 + q], self.r[1], over(hi, q))

        def to_far(self, src):
            return remote(src, self.two, self.s[4], self.r[4], opposite)

        def start(self):
            @pl.when(x < 3)
            def _():
                self.to_next().start()

            @pl.when(x == 3)
            def _():
                for q in range(3):
                    self.to_column(q).start()
                self.to_far(self.src.at[3]).start()

        def far(self):
            @pl.when(x < 3)
            def _():
                self.to_column(0).wait_recv()
                self.to_far(self.one).start()

        def end(self):
            self.to_far(self.one).wait_recv()

            @pl.when(x == 0)
            def _():
                self.dst[0] = self.two[...]

            for q in (1, 2, 3):
                @pl.when(x == q)
                def _(q=q):
                    remote(self.two, self.dst.at[q], self.s[5], self.end_sem(q), over(hi, 0)).start()

        def end_sem(self, q):
            return (self.r[5], self.r[6], self.r[2])[q - 1]

        def arrived(self):
            @pl.when(x > 0)
            def _():
                self.to_next().wait_recv()

            @pl.when(x == 0)
            def _():
                for q in (1, 2, 3):
                    remote(self.two, self.dst.at[q], self.s[5], self.end_sem(q), over(hi, 1)).wait_recv()

        def finish(self):
            @pl.when(x < 3)
            def _():
                self.to_next().wait_send()
                self.to_far(self.one).wait_send()

            @pl.when(x == 3)
            def _():
                for q in range(3):
                    self.to_column(q).wait_send()
                self.to_far(self.src.at[3]).wait_send()

            @pl.when(x > 0)
            def _():
                remote(self.two, self.dst.at[1], self.s[5], self.r[5], over(hi, 0)).wait_send()

    slab = Gather(w, ag_s, ag_r)
    rows2 = Gather(w2, bg_s, bg_r)
    states = Relay(st, nst, st1, st2, 0)
    grads = Relay(gp, ngp, gp1, gp2, 8)

    slab.issue(0)
    slab.lines()

    row_p = lax.broadcasted_iota(I32, (PR, RB), 0)
    col_p = lax.broadcasted_iota(I32, (PR, RB), 1)
    gap0 = jnp.where(row_p < PC, col_p - row_p, -4096)
    gap1 = jnp.where((row_p >= PC) & (row_p < 2 * PC), col_p - row_p + PC, -4096)

    def pick_step(n, carry):
        writer = ((n // 2) % 4) * 8 + (n // 8) * 2 + n % 2
        a = jnp.int32(-1)
        b = jnp.int32(-1)
        for j in range(8):
            s = sources[0, writer, j]
            here = (s >= 0) & (lax.shift_right_arithmetic(s, 4) == f)
            piece = jnp.bitwise_and(s, 15)
            b = jnp.where(here & (a >= 0), piece, b)
            a = jnp.where(here & (a < 0), piece, a)
        pick[n] = ((gap0 == a * PC) | (gap1 == b * PC)).astype(F32).astype(BF16)
        return carry

    row_m = lax.broadcasted_iota(I32, (SR, 4 * PR), 0)
    col_m = lax.broadcasted_iota(I32, (SR, 4 * PR), 1)
    gap_m = jnp.where(row_m < PC, col_m - row_m, -4096)

    def merge_step(zz, carry):
        writer = idx(zz, y, c)
        entry = [sources[0, writer, j] for j in range(8)]
        owner = [lax.shift_right_arithmetic(s, 4) for s in entry]
        for j in range(8):
            rank = jnp.int32(0)
            for i in range(j):
                rank = rank + jnp.where(owner[i] == owner[j], 1, 0)
            good = (entry[j] >= 0) & (lax.shift_right_arithmetic(owner[j], 3) == z)
            start = jnp.bitwise_and(lax.shift_right_arithmetic(owner[j], 1), 3) * PR + rank * PC
            same = jnp.bitwise_and(owner[j], 1) == c
            t0 = jnp.where(good & same, start, -2048)
            t1 = jnp.where(good & jnp.logical_not(same), start, -2048)
            merge[zz, 0, pl.ds(j * SR, SR), :] = (gap_m == t0).astype(F32).astype(BF16)
            merge[zz, 1, pl.ds(j * SR, SR), :] = (gap_m == t1).astype(F32).astype(BF16)
        return carry

    lax.fori_loop(0, 16, pick_step, 0)
    loads[0].wait()
    transpose_some(0, 6)
    slab.issue(1)
    slab.forward(0)
    lax.fori_loop(16, 32, pick_step, 0)
    lax.fori_loop(0, 4, merge_step, 0)
    transpose_some(6, 12)
    slab.issue(2)
    slab.last(0)
    slab.forward(1)

    def swap_copy():
        return remote(w.at[rows_of(f), :], w2.at[rows_of(4 * h + f % 4), :], pe_s, pe_r, swapped)

    @pl.when(moves)
    def _():
        swap_copy().start()

    @pl.when(jnp.logical_not(moves))
    def _():
        w2[rows_of(f), :] = w[rows_of(f), :]

    transpose_some(12, 20)
    slab.issue(3)
    loads[1].wait()
    loads[2].wait()
    for q in range(4):
        part = pl.ds(q * QS, QR)
        st[q, 0] = param[part, :].astype(BF16)
        st[q, 1] = first[part, :].astype(BF16)
        st[q, 2] = second[part, :].astype(BF16)
    states.start()
    slab.last(1)
    slab.forward(2)
    transpose_some(20, 29)
    slab.last(2)
    slab.forward(3)

    slab.last(3)

    @pl.when(moves)
    def _():
        swap_copy().wait_recv()

    rows2.lines()
    rows2.issue(0)
    for k in range(4):
        slab.wait_core(k)

    def pre_all(k, acc_):
        cols = pl.ds(pl.multiple_of(k * 8 * RB, 128), 8 * RB)
        return acc_ + jnp.dot(tok[:, cols], w[cols, :], preferred_element_type=F32)

    pre = lax.fori_loop(0, 4, pre_all, jnp.zeros((TOK, CB), F32))
    dz_own[...] = (out_grad[...].astype(F32) * gelu_slope(pre)).astype(BF16)

    for copy in slab.sent:
        copy.wait_send()

    @pl.when(moves)
    def _():
        swap_copy().wait_send()

    swap = []
    for s, k in enumerate((3, 2, 1, 0)):
        def partner_block(j, carry, k=k, s=s):
            w[rows_of(s * 4 + j), :] = jnp.dot(
                tokT[rows_of(idx(zk[k], j, 1 - c)), :], dz_own[...], preferred_element_type=F32
            ).astype(BF16)
            return carry

        lax.fori_loop(0, 4, partner_block, 0)
        area = pl.ds(s * 4 * RB, 4 * RB)
        swap.append(send(w.at[area, :], rxp.at[area, :], rs_s.at[s], rs_r.at[s], partner))
    dz_far = send(dz_own, dz_all.at[h], dz_s.at[0], dz_r.at[0], opposite)
    dz_all[h] = dz_own[...]

    def chip_block(k, s, yy):
        mine = jnp.dot(tokT[rows_of(idx(zk[k], yy, c)), :], dz_own[...], preferred_element_type=F32)
        return mine + rxp[rows_of(s * 4 + yy), :].astype(F32)

    hsend = []
    for s, k in enumerate((3, 2, 1, 0)):
        swap[s].wait_recv()
        sendh[s] = chip_block(k, s, yo).astype(BF16)
        one = send(sendh.at[s, pl.ds(0, HA)], rxh.at[s, pl.ds(0, HA)], rs_s.at[4 + s], rs_r.at[4 + s], right)
        two = send(
            sendh.at[s, pl.ds(HA, RB - HA)], rxh.at[s, pl.ds(HA, RB - HA)], rs_s.at[8 + s], rs_r.at[8 + s], left
        )
        hsend.append((one, two))

    states.far()
    fsend = []
    zout = []

    def full(s, k):
        mine = chip_block(k, s, yr)
        hsend[s][0].wait_recv()
        sendf[s, 0, pl.ds(0, HA)] = (mine[:HA] + rxh[s, pl.ds(0, HA)].astype(F32)).astype(BF16)
        sendf[s, 0, pl.ds(HA, RB - HA)] = mine[HA:].astype(BF16)
        one = send(sendf.at[s, 0], rxf.at[s, 0], rs_s.at[12 + s], rs_r.at[12 + s], right)
        mine = chip_block(k, s, yl)
        hsend[s][1].wait_recv()
        sendf[s, 1, pl.ds(0, HA)] = mine[:HA].astype(BF16)
        sendf[s, 1, pl.ds(HA, RB - HA)] = (mine[HA:] + rxh[s, pl.ds(HA, RB - HA)].astype(F32)).astype(BF16)
        two = send(sendf.at[s, 1], rxf.at[s, 1], rs_s.at[16 + s], rs_r.at[16 + s], left)
        fsend.append((one, two))

    def ring_sum(s, k):
        mine = chip_block(k, s, y)
        fsend[s][0].wait_recv()
        fsend[s][1].wait_recv()
        return mine + rxf[s, 0].astype(F32) + rxf[s, 1].astype(F32)

    def line(s, k):
        sendz[s] = ring_sum(s, k).astype(BF16)
        zout.append(send(sendz.at[s], rxz.at[s], rs_s.at[20 + s], rs_r.at[20 + s], line_to[k]))

    full(0, 3)
    full(1, 2)
    dz_far.wait_recv()
    dz_x = []
    for i, to in enumerate(xs):
        dz_x.append(send(dz_own, dz_all.at[h], dz_s.at[1 + i], dz_r.at[1 + i], to))
        other = (1 - hi) * 4 + x
        dz_x.append(send(dz_all.at[other], dz_all.at[other], dz_s.at[4 + i], dz_r.at[4 + i], to))
    line(0, 3)
    full(2, 1)
    states.end()
    line(1, 2)
    full(3, 0)
    rows2.forward(0)
    rows2.issue(1)
    line(2, 1)
    total = ring_sum(3, 0)
    for s in range(3):
        zout[s].wait_recv()
        total = total + rxz[s].astype(F32)

    grad[...] = total * (1.0 / 90.50966799187809)
    for q in range(4):
        gp[q] = grad[pl.ds(q * QS, QR), :].astype(BF16)
    grads.start()
    updated, moment, spread = adam_step(param[...], first[...], second[...], grad[...])
    new_state[0] = updated
    new_state[1] = moment
    new_state[2] = spread
    p16[...] = updated.astype(BF16)

    ysend = {}
    for k in (3, 2, 1, 0):
        zz = zk[k]

        def offer_step(yy, carry, zz=zz):
            sel = pick[pl.ds(yy * 8 + zz * 2, 2)].reshape(2 * PR, RB)
            offer[yy, zz] = jnp.dot(sel, p16[...], preferred_element_type=F32).astype(BF16)
            return carry

        lax.fori_loop(0, 4, offer_step, 0)
        taken[y, zz] = offer[y, zz]
        for i, (yy, to) in enumerate(((yr, right), (yl, left), (yo, across))):
            ysend[k, i] = send(offer.at[yy, zz], taken.at[y, zz], wr_s.at[k * 4 + i], wr_r.at[k * 4 + i], to)
    rows2.last(0)
    rows2.issue(2)
    csend = {}
    for k in (3, 2, 1, 0):
        for i in range(3):
            ysend[k, i].wait_recv()
        src = taken.at[:, zk[k], pl.ds(pl.multiple_of((1 - c) * PR, PR), PR), :]
        csend[k] = send(src, taken2.at[zk[k]], wr_s.at[k * 4 + 3], wr_r.at[k * 4 + 3], partner)
    grads.far()
    msend = {}
    for k in (3, 2, 1, 0):
        csend[k].wait_recv()
        zz = zk[k]
        mine = taken[:, zz, pl.ds(pl.multiple_of(c * PR, PR), PR), :].reshape(4 * PR, CB)
        other = taken2[zz].reshape(4 * PR, CB)
        both = jnp.dot(merge[zz, 0], mine, preferred_element_type=F32) + jnp.dot(
            merge[zz, 1], other, preferred_element_type=F32
        )
        merged[k] = both.astype(BF16)
        if k:
            msend[k] = send(merged.at[k], rxm.at[k], wr_s.at[16 + k], wr_r.at[16 + k], line_to[k])

    rows2.forward(1)
    rows2.issue(3)
    grads.end()
    for copy in dz_x:
        copy.wait_recv()

    def columns_of(k, first_one):
        rows2.wait_core(k)
        for half in range(2):
            hh = 2 * zk[k] + half
            term = dot_t(dz_all[hh], w2[pl.ds(pl.multiple_of(hh * IG, 16), IG), :])
            if first_one and half == 0:
                acc[...] = term
            else:
                acc[...] += term

    rows2.last(1)
    rows2.forward(2)
    columns_of(0, True)
    rows2.forward(3)
    rows2.last(2)
    columns_of(1, False)
    states.arrived()
    grads.arrived()
    for q in range(4):
        n = QR if q == 3 else QS
        u, m, v = adam_step(
            nst[q, 0, :n].astype(F32), nst[q, 1, :n].astype(F32), nst[q, 2, :n].astype(F32), ngp[q, :n].astype(F32)
        )
        backup[0, pl.ds(q * QS, n)] = u
        backup[1, pl.ds(q * QS, n)] = m
        backup[2, pl.ds(q * QS, n)] = v
    columns_of(2, False)
    rows2.last(3)
    columns_of(3, False)
    input_grad[...] = acc[...].astype(BF16)
    for k in (1, 2, 3):
        msend[k].wait_recv()
    for j in range(8):
        rows = pl.ds(j * SR, SR)
        piece = (merged[0, rows].astype(F32) + rxm[1, rows].astype(F32)) + (
            rxm[2, rows].astype(F32) + rxm[3, rows].astype(F32)
        )
        written[0, 0, j] = piece[:PC]
    states.finish()
    grads.finish()
    for copy in rows2.sent + pending:
        copy.wait_send()


def kernel_call(*args):
    vmem = pl.BlockSpec(memory_space=pltpu.VMEM)
    hbm = pl.BlockSpec(memory_space=pl.ANY)
    dma = pltpu.SemaphoreType.DMA
    V = pltpu.VMEM
    return pl.pallas_call(
        kernel,
        name="slab",
        out_shape=(
            jax.ShapeDtypeStruct((TOK, IG), BF16),
            jax.ShapeDtypeStruct((3, RB, CB), F32),
            jax.ShapeDtypeStruct((3, RB, CB), F32),
            jax.ShapeDtypeStruct((1, 1, 8, PC, CB), F32),
        ),
        in_specs=[hbm, vmem, vmem, hbm, hbm, pl.BlockSpec(memory_space=pltpu.SMEM)],
        out_specs=(vmem,) * 4,
        scratch_shapes=[
            V((TOK, DM), BF16), V((DM, TOK), BF16), V((DM, CB), BF16), V((DM, CB), BF16),
            V((16 * RB, CB), BF16), V((4, RB, CB), BF16), V((4, RB, CB), BF16),
            V((4, 2, RB, CB), BF16), V((4, 2, RB, CB), BF16), V((3, RB, CB), BF16), V((3, RB, CB), BF16),
            V((TOK, CB), BF16), V((8, TOK, CB), BF16),
            V((RB, CB), F32), V((RB, CB), F32),
            V((4, 3, QR, CB), BF16), V((4, 3, QR, CB), BF16), V((3, QR, CB), BF16), V((3, QR, CB), BF16),
            V((4, QR, CB), BF16), V((4, QR, CB), BF16), V((QR, CB), BF16), V((QR, CB), BF16),
            V((TOK, IG), F32), V((RB, CB), F32), V((RB, CB), BF16),
            V((32, PR, RB), BF16), V((4, 2, 8 * SR, 4 * PR), BF16),
            V((4, 4, 2 * PR, CB), BF16), V((4, 4, 2 * PR, CB), BF16), V((4, 4, PR, CB), BF16),
            V((4, 8 * SR, CB), BF16), V((4, 8 * SR, CB), BF16),
            dma((3,)), dma((36,)), dma((36,)), dma((36,)), dma((36,)), dma((24,)), dma((24,)),
            dma((7,)), dma((7,)), dma, dma, dma((16,)), dma((16,)), dma((20,)), dma((20,)),
        ],
        compiler_params=pltpu.CompilerParams(
            collective_id=0, has_side_effects=True, vmem_limit_bytes=62 * 1024 * 1024
        ),
        cost_estimate=pl.CostEstimate(
            flops=6 * TOK * DM * CB, bytes_accessed=20_000_000, transcendentals=2 * TOK * CB
        ),
    )(*args)


def on_device(tokens, out_grad, param, first, second, sources):
    return kernel_call(tokens, out_grad, param, first, second, sources)


def solution(mesh):
    return jax.shard_map(
        on_device,
        mesh=mesh,
        in_specs=(
            P("fsdp", None),
            P("fsdp", "hst"),
            P("fsdp", "hst"),
            P("fsdp", "hst"),
            P("fsdp", "hst"),
            P("hst", None, None),
        ),
        out_specs=(
            P("fsdp", "hst"),
            P(None, "fsdp", "hst"),
            P(None, "fsdp", "hst"),
            P("hst", "fsdp", None, None, None),
        ),
        check_vma=False,
    )
```

```python
import functools

import jax
import jax.numpy as jnp
from jax import lax
from jax.experimental import pallas as pl
from jax.experimental.pallas import tpu as pltpu
from jax.sharding import PartitionSpec as P

MESH = pl.DeviceIdType.MESH
BF16 = jnp.bfloat16
F32 = jnp.float32
I32 = jnp.int32
TOK = 256
RB = 464
CB = 256
DM = 32 * RB
IG = DM // 8
HA = 240
PC = 29
PR = 64
SR = 32
QS, QR = 112, 128


def gelu_slope(pre):
    cdf = 0.5 * (1.0 + lax.erf(pre * 0.7071067811865476))
    pdf = jnp.exp(-0.5 * pre * pre) * 0.3989422804014327
    return cdf + pre * pdf


def adam_step(param, first, second, grad):
    moment = 0.8 * first + 0.2 * grad
    spread = 0.9 * second + 0.1 * grad * grad
    updated = param - 0.1 * (moment / (jnp.sqrt(spread) + 1e-08) + 0.1 * param)
    return (updated, moment, spread)


def rows_of(f):
    return pl.ds(pl.multiple_of(f * RB, 16), RB)


def dot_t(a, b):
    return lax.dot_general(a, b, (((1,), (1,)), ((), ())), preferred_element_type=F32)


def kernel(
    tokens, out_grad, param, first_in, second_in, sources,
    input_grad, new_state, backup, written,
    tok, tokT, w, w2, rxp, sendh, rxh, sendf, rxf, sendz, rxz, dz_own, dz_all,
    first, second, st, nst, st1, st2, gp, ngp, gp1, gp2, acc, grad, p16,
    pick, merge, offer, taken, taken2, merged, rxm,
    xc_s, xc_r, in_sem, ag_s, ag_r, bg_s, bg_r, rs_s, rs_r, dz_s, dz_r, pe_s, pe_r, re_s, re_r, wr_s, wr_r,
):
    f = lax.axis_index("fsdp")
    h = lax.axis_index("hst")
    z, y, c = f // 8, (f // 2) % 4, f % 2
    hi, x = h // 4, h % 4
    yr, yl, yo = (y + 1) % 4, (y + 3) % 4, (y + 2) % 4
    near = z + 1 - 2 * (z % 2)
    zx = [z, near, (z + 2) % 4, 3 - z]
    zk = [z, near, 2 - z // 2, 3 - 3 * (z // 2)]
    inner = (z == 1) | (z == 2)

    def idx(zz, yy, cc):
        return zz * 8 + yy * 2 + cc

    def at(zz, yy, cc):
        return {"fsdp": idx(zz, yy, cc)}

    def over(ww, xx):
        return {"hst": ww * 4 + xx}

    right, left, partner, across = at(z, yr, c), at(z, yl, c), at(z, y, 1 - c), at(z, yo, c)
    line_to = [None] + [at(zx[k], y, c) for k in (1, 2, 3)]
    opposite = over(1 - hi, x)
    xs = [over(hi, (x + i) % 4) for i in (1, 2, 3)]
    swapped = {"fsdp": 4 * h + f % 4, "hst": f // 4}
    member = (z // 2 + hi) % 2
    moves = member == 1
    stays = member == 0
    order2 = [member * z + (1 - member) * (2 - hi), member * near + (1 - member) * (3 - 3 * hi)]

    loads = [
        pltpu.make_async_copy(a, b, in_sem.at[i])
        for i, (a, b) in enumerate(((tokens, tok), (first_in, first), (second_in, second)))
    ]
    for load in loads:
        load.start()
    w[rows_of(f), :] = param[...].astype(BF16)

    barrier = pltpu.get_barrier_semaphore()
    for peer in (right, left, across, partner, *line_to[1:], opposite, *xs):
        pl.semaphore_signal(barrier, inc=1, device_id=peer, device_id_type=MESH)

    @pl.when(moves)
    def _():
        pl.semaphore_signal(barrier, inc=1, device_id=swapped, device_id_type=MESH)
        pl.semaphore_wait(barrier, 12)

    @pl.when(stays)
    def _():
        pl.semaphore_wait(barrier, 11)

    pending = []

    def remote(src, dst, s_sem, r_sem, to):
        return pltpu.make_async_remote_copy(
            src_ref=src, dst_ref=dst, send_sem=s_sem, recv_sem=r_sem, device_id=to, device_id_type=MESH
        )

    def send(src, dst, s_sem, r_sem, to):
        copy = remote(src, dst, s_sem, r_sem, to)
        copy.start()
        pending.append(copy)
        return copy

    class Gather:
        def __init__(self, buf, s_sem, r_sem, order):
            self.buf, self.s, self.r, self.zk = buf, s_sem, r_sem, order
            self.own, self.core, self.halves = {}, {}, {}
            self.sent, self.some, self.came = [], [], set()

        def copy(self, block, lo, n, s_sem, r_sem, to):
            ref = self.buf.at[pl.ds(pl.multiple_of(block * RB + lo, 16), n), :]
            return remote(ref, ref, self.s.at[s_sem], self.r.at[r_sem], to)

        def put(self, block, lo, n, sem, to):
            copy = self.copy(block, lo, n, sem, sem, to)
            copy.start()
            self.sent.append(copy)
            return copy

        def put_some(self, cond, block, s_sem, r_sem, to):
            copy = self.copy(block, 0, RB, s_sem, r_sem, to)
            pl.when(cond)(copy.start)
            self.some.append((cond, copy))

        def lines(self):
            self.put_some(z >= 0, f, 33, 33, line_to[1])
            self.put_some(inner, f, 34, 34, line_to[3])

        def arrive(self, k):
            self.came.add(k)
            if k == 0:
                return
            b = idx(self.zk[k], y, c)
            self.copy(b, 0, RB, 33, 32 + k, line_to[1]).wait_recv()
            self.put_some(inner, b, 34 + k, (35, 34, 35)[k - 1], (line_to[3], line_to[1], line_to[1])[k - 1])

        def issue(self, k):
            self.arrive(k)
            b = idx(self.zk[k], y, c)
            self.own[k] = (self.put(b, 0, RB, k * 8, right), self.put(b, 0, RB, k * 8 + 1, left))
            self.core[k, 0] = self.put(b, 0, RB, k * 8 + 4, partner)

        def forward(self, k):
            self.own[k][0].wait_recv()
            b = idx(self.zk[k], yl, c)
            one = self.put(b, 0, HA, k * 8 + 2, right)
            self.core[k, 1] = self.put(b, 0, RB, k * 8 + 5, partner)
            self.own[k][1].wait_recv()
            b = idx(self.zk[k], yr, c)
            two = self.put(b, HA, RB - HA, k * 8 + 3, left)
            self.core[k, 2] = self.put(b, 0, RB, k * 8 + 6, partner)
            self.halves[k] = (one, two)

        def last(self, k):
            self.halves[k][0].wait_recv()
            self.halves[k][1].wait_recv()
            self.core[k, 3] = self.put(idx(self.zk[k], yo, c), 0, RB, k * 8 + 7, partner)

        def wait_core(self, k):
            for j in range(4):
                self.core[k, j].wait_recv()

        def finish(self):
            for copy in self.sent:
                copy.wait_send()
            for cond, copy in self.some:
                pl.when(cond)(copy.wait_send)

    class HalfGather(Gather):
        def lines(self):
            self.put_some(moves, f, 33, 34, line_to[1])
            self.put_some(moves & inner, f, 34, 33, line_to[3])

        def arrive(self, k):
            self.came.add(k)
            b = idx(self.zk[k], y, c)
            came = self.copy(b, 0, RB, 33, 33 + k, line_to[1])
            if k == 0:
                pl.when(stays)(came.wait_recv)
                self.put_some(stays & inner, b, 35, 33, line_to[1])
            else:
                came.wait_recv()
                self.put_some(moves & inner, b, 36, 34, line_to[3])
                self.put_some(stays & inner, b, 37, 34, line_to[1])

    def transpose_some(lo, hi_):
        def step(i, carry):
            cols = pl.ds(pl.multiple_of(i * 512, 512), 512)
            tokT[cols, :] = tok[:, cols].T
            return carry

        lax.fori_loop(lo, hi_, step, 0)

    class Relay:
        def __init__(self, src, dst, one, two, sem):
            self.src, self.dst, self.one, self.two = src, dst, one, two
            self.s = [re_s.at[sem + i] for i in range(7)]
            self.r = [re_r.at[sem + i] for i in range(7)]

        def to_next(self):
            return remote(self.src, self.dst, self.s[0], self.r[0], over(hi, (x + 1) % 4))

        def to_column(self, q):
            return remote(self.src.at[q], self.one, self.s[1 + q], self.r[1], over(hi, q))

        def to_far(self, src):
            return remote(src, self.two, self.s[4], self.r[4], opposite)

        def start(self):
            @pl.when(x < 3)
            def _():
                self.to_next().start()

            @pl.when(x == 3)
            def _():
                for q in range(3):
                    self.to_column(q).start()
                self.to_far(self.src.at[3]).start()

        def far(self):
            @pl.when(x < 3)
            def _():
                self.to_column(0).wait_recv()
                self.to_far(self.one).start()

        def end(self):
            self.to_far(self.one).wait_recv()

            @pl.when(x == 0)
            def _():
                self.dst[0] = self.two[...]

            for q in (1, 2, 3):
                @pl.when(x == q)
                def _(q=q):
                    remote(self.two, self.dst.at[q], self.s[5], self.end_sem(q), over(hi, 0)).start()

        def end_sem(self, q):
            return (self.r[5], self.r[6], self.r[2])[q - 1]

        def arrived(self):
            @pl.when(x > 0)
            def _():
                self.to_next().wait_recv()

            @pl.when(x == 0)
            def _():
                for q in (1, 2, 3):
                    remote(self.two, self.dst.at[q], self.s[5], self.end_sem(q), over(hi, 1)).wait_recv()

        def finish(self):
            @pl.when(x < 3)
            def _():
                self.to_next().wait_send()
                self.to_far(self.one).wait_send()

            @pl.when(x == 3)
            def _():
                for q in range(3):
                    self.to_column(q).wait_send()
                self.to_far(self.src.at[3]).wait_send()

            @pl.when(x > 0)
            def _():
                remote(self.two, self.dst.at[1], self.s[5], self.r[5], over(hi, 0)).wait_send()

    slab = Gather(w, ag_s, ag_r, zk)
    rows2 = HalfGather(w2, bg_s, bg_r, order2)
    states = Relay(st, nst, st1, st2, 0)
    grads = Relay(gp, ngp, gp1, gp2, 8)

    slab.lines()
    slab.issue(0)

    row_p = lax.broadcasted_iota(I32, (PR, RB), 0)
    col_p = lax.broadcasted_iota(I32, (PR, RB), 1)
    gap0 = jnp.where(row_p < PC, col_p - row_p, -4096)
    gap1 = jnp.where((row_p >= PC) & (row_p < 2 * PC), col_p - row_p + PC, -4096)

    def pick_step(n, carry):
        writer = ((n // 2) % 4) * 8 + (n // 8) * 2 + n % 2
        a = jnp.int32(-1)
        b = jnp.int32(-1)
        for j in range(8):
            s = sources[0, j, writer]
            here = (s >= 0) & (lax.shift_right_arithmetic(s, 4) == f)
            piece = jnp.bitwise_and(s, 15)
            b = jnp.where(here & (a >= 0), piece, b)
            a = jnp.where(here & (a < 0), piece, a)
        pick[n] = ((gap0 == a * PC) | (gap1 == b * PC)).astype(F32).astype(BF16)
        return carry

    row_m = lax.broadcasted_iota(I32, (SR, 4 * PR), 0)
    col_m = lax.broadcasted_iota(I32, (SR, 4 * PR), 1)
    gap_m = jnp.where(row_m < PC, col_m - row_m, -4096)

    def merge_step(zz, carry):
        writer = idx(zz, y, c)
        entry = [sources[0, j, writer] for j in range(8)]
        owner = [lax.shift_right_arithmetic(s, 4) for s in entry]
        for j in range(8):
            rank = jnp.int32(0)
            for i in range(j):
                rank = rank + jnp.where(owner[i] == owner[j], 1, 0)
            good = (entry[j] >= 0) & (lax.shift_right_arithmetic(owner[j], 3) == z)
            start = jnp.bitwise_and(lax.shift_right_arithmetic(owner[j], 1), 3) * PR + rank * PC
            same = jnp.bitwise_and(owner[j], 1) == c
            t0 = jnp.where(good & same, start, -2048)
            t1 = jnp.where(good & jnp.logical_not(same), start, -2048)
            merge[zz, 0, pl.ds(j * SR, SR), :] = (gap_m == t0).astype(F32).astype(BF16)
            merge[zz, 1, pl.ds(j * SR, SR), :] = (gap_m == t1).astype(F32).astype(BF16)
        return carry

    lax.fori_loop(0, 16, pick_step, 0)
    loads[0].wait()
    transpose_some(0, 6)
    slab.issue(1)

    def swap_copy():
        return remote(w.at[rows_of(f), :], w2.at[rows_of(4 * h + f % 4), :], pe_s, pe_r, swapped)

    @pl.when(moves)
    def _():
        swap_copy().start()

    slab.forward(0)
    lax.fori_loop(16, 32, pick_step, 0)
    lax.fori_loop(0, 4, merge_step, 0)
    transpose_some(6, 12)
    slab.issue(2)
    slab.last(0)
    slab.forward(1)

    transpose_some(12, 20)
    slab.issue(3)
    loads[1].wait()
    loads[2].wait()
    for q in range(4):
        part = pl.ds(q * QS, QR)
        st[q, 0] = param[part, :].astype(BF16)
        st[q, 1] = first[part, :].astype(BF16)
        st[q, 2] = second[part, :].astype(BF16)
    states.start()
    slab.last(1)
    slab.forward(2)
    transpose_some(20, 29)
    slab.last(2)

    @pl.when(moves)
    def _():
        swap_copy().wait_recv()

    rows2.lines()
    slab.forward(3)
    rows2.issue(0)

    slab.last(3)

    rows2.issue(1)

    xcopies = {}
    for i, to in enumerate(xs):
        row = 4 * (4 * hi + (x + 1 + i) % 4) + c
        for b in range(2):
            xcopies[i, b] = send(
                w.at[rows_of(row + 2 * b), :], w2.at[rows_of(4 * h + 2 * b + c), :],
                xc_s.at[2 * i + b], xc_r.at[2 * i + b], to,
            )
    for k in range(4):
        slab.wait_core(k)
    span = pl.ds(pl.multiple_of(h * IG, 16), IG)
    own_rows = pltpu.make_async_copy(w.at[span, :], w2.at[span, :], in_sem.at[3])
    own_rows.start()

    def pre_all(k, acc_):
        cols = pl.ds(pl.multiple_of(k * 8 * RB, 128), 8 * RB)
        return acc_ + jnp.dot(tok[:, cols], w[cols, :], preferred_element_type=F32)

    pre = lax.fori_loop(0, 4, pre_all, jnp.zeros((TOK, CB), F32))
    dz_own[...] = (out_grad[...].astype(F32) * gelu_slope(pre)).astype(BF16)

    slab.finish()

    @pl.when(moves)
    def _():
        swap_copy().wait_send()

    swap = []
    for s, k in enumerate((3, 2, 1, 0)):
        def partner_block(j, carry, k=k, s=s):
            w[rows_of(16 * (1 - hi) + s * 4 + j), :] = jnp.dot(
                tokT[rows_of(idx(zx[k], j, 1 - c)), :], dz_own[...], preferred_element_type=F32
            ).astype(BF16)
            return carry

        lax.fori_loop(0, 4, partner_block, 0)
        area = pl.ds(s * 4 * RB, 4 * RB)
        part = pl.ds(pl.multiple_of((16 * (1 - hi) + s * 4) * RB, 16), 4 * RB)
        swap.append(send(w.at[part, :], rxp.at[area, :], rs_s.at[s], rs_r.at[s], partner))
    dz_far = send(dz_own, dz_all.at[h], dz_s.at[0], dz_r.at[0], opposite)
    dz_all[h] = dz_own[...]

    def chip_block(k, s, yy):
        mine = jnp.dot(tokT[rows_of(idx(zx[k], yy, c)), :], dz_own[...], preferred_element_type=F32)
        return mine + rxp[rows_of(s * 4 + yy), :].astype(F32)

    hsend = []

    def half(s, k):
        swap[s].wait_recv()
        sendh[s] = chip_block(k, s, yo).astype(BF16)
        one = send(sendh.at[s, pl.ds(0, HA)], rxh.at[s, pl.ds(0, HA)], rs_s.at[4 + s], rs_r.at[4 + s], right)
        two = send(
            sendh.at[s, pl.ds(HA, RB - HA)], rxh.at[s, pl.ds(HA, RB - HA)], rs_s.at[8 + s], rs_r.at[8 + s], left
        )
        hsend.append((one, two))

    fsend = []
    zout = []

    def full(s, k):
        mine = chip_block(k, s, yr)
        hsend[s][0].wait_recv()
        sendf[s, 0, pl.ds(0, HA)] = (mine[:HA] + rxh[s, pl.ds(0, HA)].astype(F32)).astype(BF16)
        sendf[s, 0, pl.ds(HA, RB - HA)] = mine[HA:].astype(BF16)
        one = send(sendf.at[s, 0], rxf.at[s, 0], rs_s.at[12 + s], rs_r.at[12 + s], right)
        mine = chip_block(k, s, yl)
        hsend[s][1].wait_recv()
        sendf[s, 1, pl.ds(0, HA)] = mine[:HA].astype(BF16)
        sendf[s, 1, pl.ds(HA, RB - HA)] = (mine[HA:] + rxh[s, pl.ds(HA, RB - HA)].astype(F32)).astype(BF16)
        two = send(sendf.at[s, 1], rxf.at[s, 1], rs_s.at[16 + s], rs_r.at[16 + s], left)
        fsend.append((one, two))

    def ring_sum(s, k):
        mine = chip_block(k, s, y)
        fsend[s][0].wait_recv()
        fsend[s][1].wait_recv()
        return mine + rxf[s, 0].astype(F32) + rxf[s, 1].astype(F32)

    def line(s, k):
        sendz[s] = ring_sum(s, k).astype(BF16)
        zout.append(send(sendz.at[s], rxz.at[s], rs_s.at[20 + s], rs_r.at[20 + s], line_to[k]))

    half(0, 3)
    half(1, 2)
    full(0, 3)
    half(2, 1)
    dz_far.wait_recv()
    dz_x = []
    for i, to in enumerate(xs):
        dz_x.append(send(dz_own, dz_all.at[h], dz_s.at[1 + i], dz_r.at[1 + i], to))
        other = (1 - hi) * 4 + x
        dz_x.append(send(dz_all.at[other], dz_all.at[other], dz_s.at[4 + i], dz_r.at[4 + i], to))
    full(1, 2)
    states.far()
    line(0, 3)
    half(3, 0)
    full(2, 1)
    line(1, 2)
    full(3, 0)
    rows2.forward(0)
    states.end()
    line(2, 1)
    total = ring_sum(3, 0)
    for s in range(3):
        zout[s].wait_recv()
        total = total + rxz[s].astype(F32)

    grad[...] = total * (1.0 / 90.50966799187809)
    for q in range(4):
        gp[q] = grad[pl.ds(q * QS, QR), :].astype(BF16)
    grads.start()
    updated, moment, spread = adam_step(param[...], first[...], second[...], grad[...])
    new_state[0] = updated
    new_state[1] = moment
    new_state[2] = spread
    p16[...] = updated.astype(BF16)

    ysend = {}
    for k in (3, 2, 1, 0):
        zz = zx[k]

        def offer_step(yy, carry, zz=zz):
            sel = pick[pl.ds(yy * 8 + zz * 2, 2)].reshape(2 * PR, RB)
            offer[yy, zz] = jnp.dot(sel, p16[...], preferred_element_type=F32).astype(BF16)
            return carry

        lax.fori_loop(0, 4, offer_step, 0)
        taken[y, zz] = offer[y, zz]
        for i, (yy, to) in enumerate(((yr, right), (yl, left), (yo, across))):
            ysend[k, i] = send(offer.at[yy, zz], taken.at[y, zz], wr_s.at[k * 4 + i], wr_r.at[k * 4 + i], to)
    rows2.forward(1)
    xcore = {}
    for i in range(3):
        for b in range(2):
            xcopies[i, b].wait_recv()
            slot = rows_of(4 * (4 * hi + (x + 3 - i) % 4) + 2 * b + c)
            xcore[i, b] = send(w2.at[slot, :], w2.at[slot, :], xc_s.at[6 + 2 * i + b], xc_r.at[6 + 2 * i + b], partner)
    csend = {}
    for k in (3, 2, 1, 0):
        for i in range(3):
            ysend[k, i].wait_recv()
        src = taken.at[:, zx[k], pl.ds(pl.multiple_of((1 - c) * PR, PR), PR), :]
        csend[k] = send(src, taken2.at[zx[k]], wr_s.at[k * 4 + 3], wr_r.at[k * 4 + 3], partner)
    grads.far()
    msend = {}
    for k in (3, 2, 1, 0):
        csend[k].wait_recv()
        zz = zx[k]
        mine = taken[:, zz, pl.ds(pl.multiple_of(c * PR, PR), PR), :].reshape(4 * PR, CB)
        other = taken2[zz].reshape(4 * PR, CB)
        both = jnp.dot(merge[zz, 0], mine, preferred_element_type=F32) + jnp.dot(
            merge[zz, 1], other, preferred_element_type=F32
        )
        merged[k] = both.astype(BF16)
        if k:
            msend[k] = send(merged.at[k], rxm.at[k], wr_s.at[16 + k], wr_r.at[16 + k], line_to[k])

    rows2.last(0)
    grads.end()
    for copy in dz_x:
        copy.wait_recv()
    own_rows.wait()

    def add_term(hh, first_one=False):
        term = dot_t(w2[pl.ds(pl.multiple_of(hh * IG, 16), IG), :], dz_all[hh])
        if first_one:
            acc[...] = term
        else:
            acc[...] += term

    add_term(h, True)
    rows2.last(1)
    for i in range(3):
        for b in range(2):
            xcore[i, b].wait_recv()
        add_term(4 * hi + (x + 3 - i) % 4)
    states.arrived()
    grads.arrived()
    for q in range(4):
        n = QR if q == 3 else QS
        u, m, v = adam_step(
            nst[q, 0, :n].astype(F32), nst[q, 1, :n].astype(F32), nst[q, 2, :n].astype(F32), ngp[q, :n].astype(F32)
        )
        backup[0, pl.ds(q * QS, n)] = u
        backup[1, pl.ds(q * QS, n)] = m
        backup[2, pl.ds(q * QS, n)] = v
    for k in range(2):
        rows2.wait_core(k)
        for half_ in range(2):
            add_term(2 * order2[k] + half_)
    input_grad[...] = acc[...].astype(BF16)
    for k in (1, 2, 3):
        msend[k].wait_recv()
    for j in range(8):
        rows = pl.ds(j * SR, SR)
        piece = (merged[0, rows].astype(F32) + rxm[1, rows].astype(F32)) + (
            rxm[2, rows].astype(F32) + rxm[3, rows].astype(F32)
        )
        written[0, 0, :, j, :] = piece[:PC]
    states.finish()
    grads.finish()
    rows2.finish()
    for copy in pending:
        copy.wait_send()


def kernel_call(*args):
    vmem = pl.BlockSpec(memory_space=pltpu.VMEM)
    hbm = pl.BlockSpec(memory_space=pl.ANY)
    dma = pltpu.SemaphoreType.DMA
    V = pltpu.VMEM
    return pl.pallas_call(
        kernel,
        name="slab",
        out_shape=(
            pltpu.VMEM((IG, TOK), BF16),
            pltpu.VMEM((3, RB, CB), F32),
            pltpu.VMEM((3, RB, CB), F32),
            pltpu.VMEM((1, 1, PC, 8, CB), F32),
        ),
        in_specs=[hbm, vmem, vmem, hbm, hbm, pl.BlockSpec(memory_space=pltpu.SMEM)],
        out_specs=(vmem,) * 4,
        scratch_shapes=[
            V((TOK, DM), BF16), V((DM, TOK), BF16), V((DM, CB), BF16), V((DM, CB), BF16),
            V((16 * RB, CB), BF16), V((4, RB, CB), BF16), V((4, RB, CB), BF16),
            V((4, 2, RB, CB), BF16), V((4, 2, RB, CB), BF16), V((3, RB, CB), BF16), V((3, RB, CB), BF16),
            V((TOK, CB), BF16), V((8, TOK, CB), BF16),
            V((RB, CB), F32), V((RB, CB), F32),
            V((4, 3, QR, CB), BF16), V((4, 3, QR, CB), BF16), V((3, QR, CB), BF16), V((3, QR, CB), BF16),
            V((4, QR, CB), BF16), V((4, QR, CB), BF16), V((QR, CB), BF16), V((QR, CB), BF16),
            V((IG, TOK), F32), V((RB, CB), F32), V((RB, CB), BF16),
            V((32, PR, RB), BF16), V((4, 2, 8 * SR, 4 * PR), BF16),
            V((4, 4, 2 * PR, CB), BF16), V((4, 4, 2 * PR, CB), BF16), V((4, 4, PR, CB), BF16),
            V((4, 8 * SR, CB), BF16), V((4, 8 * SR, CB), BF16),
            dma((12,)), dma((12,)), dma((8,)), dma((38,)), dma((38,)), dma((38,)), dma((38,)), dma((24,)), dma((24,)),
            dma((7,)), dma((7,)), dma, dma, dma((16,)), dma((16,)), dma((20,)), dma((20,)),
        ],
        compiler_params=pltpu.CompilerParams(
            collective_id=0, has_side_effects=True, vmem_limit_bytes=58 * 1024 * 1024
        ),
        cost_estimate=pl.CostEstimate(
            flops=6 * TOK * DM * CB, bytes_accessed=20_000_000, transcendentals=2 * TOK * CB
        ),
    )(*args)


def on_device(tokens, out_grad, param, first, second, sources):
    input_grad, new_state, backup, written = kernel_call(
        tokens, out_grad, param, first, second, sources.transpose(0, 2, 1)
    )
    return (input_grad.T, new_state, backup, written.transpose(0, 1, 3, 2, 4))


def solution(mesh):
    return jax.shard_map(
        on_device,
        mesh=mesh,
        in_specs=(
            P("fsdp", None),
            P("fsdp", "hst"),
            P("fsdp", "hst"),
            P("fsdp", "hst"),
            P("fsdp", "hst"),
            P("hst", None, None),
        ),
        out_specs=(
            P("fsdp", "hst"),
            P(None, "fsdp", "hst"),
            P(None, "fsdp", "hst"),
            P("hst", "fsdp", None, None, None),
        ),
        check_vma=False,
    )
```

```python
import functools

import jax
import jax.numpy as jnp
from jax import lax
from jax.experimental import pallas as pl
from jax.experimental.pallas import tpu as pltpu
from jax.sharding import PartitionSpec as P

MESH = pl.DeviceIdType.MESH
BF16 = jnp.bfloat16
F32 = jnp.float32
I32 = jnp.int32
TOK = 256
RB = 464
CB = 256
DM = 32 * RB
IG = DM // 8
HA = 240
PC = 29
PR = 64
SR = 32
QS, QR = 112, 128


def gelu_slope(pre):
    cdf = 0.5 * (1.0 + lax.erf(pre * 0.7071067811865476))
    pdf = jnp.exp(-0.5 * pre * pre) * 0.3989422804014327
    return cdf + pre * pdf


def adam_step(param, first, second, grad):
    moment = 0.8 * first + 0.2 * grad
    spread = 0.9 * second + 0.1 * grad * grad
    updated = param - 0.1 * (moment / (jnp.sqrt(spread) + 1e-08) + 0.1 * param)
    return (updated, moment, spread)


def rows_of(f):
    return pl.ds(pl.multiple_of(f * RB, 16), RB)


def dot_t(a, b):
    return lax.dot_general(a, b, (((1,), (1,)), ((), ())), preferred_element_type=F32)


def kernel(
    tokens, out_grad, param, first_in, second_in, sources,
    input_grad, new_state, backup, written,
    tok, tokT, w, w2, rxp, sendh, rxh, sendf, rxf, sendz, rxz, dz_own, dz_all,
    first, second, st, nst, st1, st2, gp, ngp, gp1, gp2, acc, grad, p16,
    pick, merge, offer, taken, taken2, merged, rxm,
    xc_s, xc_r, in_sem, ag_s, ag_r, bg_s, bg_r, rs_s, rs_r, dz_s, dz_r, pe_s, pe_r, re_s, re_r, wr_s, wr_r,
):
    f = lax.axis_index("fsdp")
    h = lax.axis_index("hst")
    z, y, c = f // 8, (f // 2) % 4, f % 2
    hi, x = h // 4, h % 4
    yr, yl, yo = (y + 1) % 4, (y + 3) % 4, (y + 2) % 4
    near = z + 1 - 2 * (z % 2)
    zx = [z, near, (z + 2) % 4, 3 - z]
    zk = [z, near, 2 - z // 2, 3 - 3 * (z // 2)]
    inner = (z == 1) | (z == 2)

    def idx(zz, yy, cc):
        return zz * 8 + yy * 2 + cc

    def at(zz, yy, cc):
        return {"fsdp": idx(zz, yy, cc)}

    def over(ww, xx):
        return {"hst": ww * 4 + xx}

    right, left, partner, across = at(z, yr, c), at(z, yl, c), at(z, y, 1 - c), at(z, yo, c)
    line_to = [None] + [at(zx[k], y, c) for k in (1, 2, 3)]
    opposite = over(1 - hi, x)
    xs = [over(hi, (x + i) % 4) for i in (1, 2, 3)]
    swapped = {"fsdp": 4 * h + f % 4, "hst": f // 4}
    member = (z // 2 + hi) % 2
    moves = member == 1
    stays = member == 0
    order2 = [member * z + (1 - member) * (2 - hi), member * near + (1 - member) * (3 - 3 * hi)]

    loads = [
        pltpu.make_async_copy(a, b, in_sem.at[i])
        for i, (a, b) in enumerate(((tokens, tok), (first_in, first), (second_in, second)))
    ]
    for load in loads:
        load.start()

    barrier = pltpu.get_barrier_semaphore()
    for peer in (right, left, across, partner, *line_to[1:], opposite, *xs):
        pl.semaphore_signal(barrier, inc=1, device_id=peer, device_id_type=MESH)

    @pl.when(moves)
    def _():
        pl.semaphore_signal(barrier, inc=1, device_id=swapped, device_id_type=MESH)

    w[rows_of(f), :] = param[...].astype(BF16)

    @pl.when(moves)
    def _():
        pl.semaphore_wait(barrier, 12)

    @pl.when(stays)
    def _():
        pl.semaphore_wait(barrier, 11)

    pending = []

    def remote(src, dst, s_sem, r_sem, to):
        return pltpu.make_async_remote_copy(
            src_ref=src, dst_ref=dst, send_sem=s_sem, recv_sem=r_sem, device_id=to, device_id_type=MESH
        )

    def send(src, dst, s_sem, r_sem, to):
        copy = remote(src, dst, s_sem, r_sem, to)
        copy.start()
        pending.append(copy)
        return copy

    class Gather:
        def __init__(self, buf, s_sem, r_sem, order):
            self.buf, self.s, self.r, self.zk = buf, s_sem, r_sem, order
            self.own, self.core, self.halves = {}, {}, {}
            self.sent, self.some, self.came = [], [], set()

        def copy(self, block, lo, n, s_sem, r_sem, to):
            ref = self.buf.at[pl.ds(pl.multiple_of(block * RB + lo, 16), n), :]
            return remote(ref, ref, self.s.at[s_sem], self.r.at[r_sem], to)

        def put(self, block, lo, n, sem, to):
            copy = self.copy(block, lo, n, sem, sem, to)
            copy.start()
            self.sent.append(copy)
            return copy

        def put_some(self, cond, block, s_sem, r_sem, to):
            copy = self.copy(block, 0, RB, s_sem, r_sem, to)
            pl.when(cond)(copy.start)
            self.some.append((cond, copy))

        def lines(self):
            self.put_some(z >= 0, f, 33, 33, line_to[1])
            self.put_some(inner, f, 34, 34, line_to[3])

        def arrive(self, k):
            self.came.add(k)
            if k == 0:
                return
            b = idx(self.zk[k], y, c)
            self.copy(b, 0, RB, 33, 32 + k, line_to[1]).wait_recv()
            self.put_some(inner, b, 34 + k, (35, 34, 35)[k - 1], (line_to[3], line_to[1], line_to[1])[k - 1])

        def issue(self, k):
            self.arrive(k)
            b = idx(self.zk[k], y, c)
            self.own[k] = (self.put(b, 0, RB, k * 8, right), self.put(b, 0, RB, k * 8 + 1, left))
            self.core[k, 0] = self.put(b, 0, RB, k * 8 + 4, partner)

        def forward(self, k):
            self.own[k][0].wait_recv()
            b = idx(self.zk[k], yl, c)
            one = self.put(b, 0, HA, k * 8 + 2, right)
            self.core[k, 1] = self.put(b, 0, RB, k * 8 + 5, partner)
            self.own[k][1].wait_recv()
            b = idx(self.zk[k], yr, c)
            two = self.put(b, HA, RB - HA, k * 8 + 3, left)
            self.core[k, 2] = self.put(b, 0, RB, k * 8 + 6, partner)
            self.halves[k] = (one, two)

        def last(self, k):
            self.halves[k][0].wait_recv()
            self.halves[k][1].wait_recv()
            self.core[k, 3] = self.put(idx(self.zk[k], yo, c), 0, RB, k * 8 + 7, partner)

        def wait_core(self, k):
            for j in range(4):
                self.core[k, j].wait_recv()

        def finish(self):
            for copy in self.sent:
                copy.wait_send()
            for cond, copy in self.some:
                pl.when(cond)(copy.wait_send)

    class HalfGather(Gather):
        def lines(self):
            self.put_some(moves, f, 33, 34, line_to[1])
            self.put_some(moves & inner, f, 34, 33, line_to[3])

        def arrive(self, k):
            self.came.add(k)
            b = idx(self.zk[k], y, c)
            came = self.copy(b, 0, RB, 33, 33 + k, line_to[1])
            if k == 0:
                pl.when(stays)(came.wait_recv)
                self.put_some(stays & inner, b, 35, 33, line_to[1])
            else:
                came.wait_recv()
                self.put_some(moves & inner, b, 36, 34, line_to[3])
                self.put_some(stays & inner, b, 37, 34, line_to[1])

    def transpose_some(lo, hi_):
        def step(i, carry):
            cols = pl.ds(pl.multiple_of(i * 512, 512), 512)
            tokT[cols, :] = tok[:, cols].T
            return carry

        lax.fori_loop(lo, hi_, step, 0)

    class Relay:
        def __init__(self, src, dst, one, two, sem):
            self.src, self.dst, self.one, self.two = src, dst, one, two
            self.s = [re_s.at[sem + i] for i in range(7)]
            self.r = [re_r.at[sem + i] for i in range(7)]

        def to_next(self):
            return remote(self.src, self.dst, self.s[0], self.r[0], over(hi, (x + 1) % 4))

        def to_column(self, q):
            return remote(self.src.at[q], self.one, self.s[1 + q], self.r[1], over(hi, q))

        def to_far(self, src):
            return remote(src, self.two, self.s[4], self.r[4], opposite)

        def start(self):
            @pl.when(x < 3)
            def _():
                self.to_next().start()

            @pl.when(x == 3)
            def _():
                for q in range(3):
                    self.to_column(q).start()
                self.to_far(self.src.at[3]).start()

        def far(self):
            @pl.when(x < 3)
            def _():
                self.to_column(0).wait_recv()
                self.to_far(self.one).start()

        def end(self):
            self.to_far(self.one).wait_recv()

            @pl.when(x == 0)
            def _():
                self.dst[0] = self.two[...]

            for q in (1, 2, 3):
                @pl.when(x == q)
                def _(q=q):
                    remote(self.two, self.dst.at[q], self.s[5], self.end_sem(q), over(hi, 0)).start()

        def end_sem(self, q):
            return (self.r[5], self.r[6], self.r[2])[q - 1]

        def arrived(self):
            @pl.when(x > 0)
            def _():
                self.to_next().wait_recv()

            @pl.when(x == 0)
            def _():
                for q in (1, 2, 3):
                    remote(self.two, self.dst.at[q], self.s[5], self.end_sem(q), over(hi, 1)).wait_recv()

        def finish(self):
            @pl.when(x < 3)
            def _():
                self.to_next().wait_send()
                self.to_far(self.one).wait_send()

            @pl.when(x == 3)
            def _():
                for q in range(3):
                    self.to_column(q).wait_send()
                self.to_far(self.src.at[3]).wait_send()

            @pl.when(x > 0)
            def _():
                remote(self.two, self.dst.at[1], self.s[5], self.r[5], over(hi, 0)).wait_send()

    slab = Gather(w, ag_s, ag_r, zk)
    rows2 = HalfGather(w2, bg_s, bg_r, order2)
    states = Relay(st, nst, st1, st2, 0)
    grads = Relay(gp, ngp, gp1, gp2, 8)

    slab.lines()
    slab.issue(0)

    row_p = lax.broadcasted_iota(I32, (PR, RB), 0)
    col_p = lax.broadcasted_iota(I32, (PR, RB), 1)
    gap0 = jnp.where(row_p < PC, col_p - row_p, -4096)
    gap1 = jnp.where((row_p >= PC) & (row_p < 2 * PC), col_p - row_p + PC, -4096)

    def pick_step(n, carry):
        writer = ((n // 2) % 4) * 8 + (n // 8) * 2 + n % 2
        a = jnp.int32(-1)
        b = jnp.int32(-1)
        for j in range(8):
            s = sources[0, j, writer]
            here = (s >= 0) & (lax.shift_right_arithmetic(s, 4) == f)
            piece = jnp.bitwise_and(s, 15)
            b = jnp.where(here & (a >= 0), piece, b)
            a = jnp.where(here & (a < 0), piece, a)
        pick[n] = ((gap0 == a * PC) | (gap1 == b * PC)).astype(F32).astype(BF16)
        return carry

    row_m = lax.broadcasted_iota(I32, (SR, 4 * PR), 0)
    col_m = lax.broadcasted_iota(I32, (SR, 4 * PR), 1)
    gap_m = jnp.where(row_m < PC, col_m - row_m, -4096)

    def merge_step(zz, carry):
        writer = idx(zz, y, c)
        entry = [sources[0, j, writer] for j in range(8)]
        owner = [lax.shift_right_arithmetic(s, 4) for s in entry]
        for j in range(8):
            rank = jnp.int32(0)
            for i in range(j):
                rank = rank + jnp.where(owner[i] == owner[j], 1, 0)
            good = (entry[j] >= 0) & (lax.shift_right_arithmetic(owner[j], 3) == z)
            start = jnp.bitwise_and(lax.shift_right_arithmetic(owner[j], 1), 3) * PR + rank * PC
            same = jnp.bitwise_and(owner[j], 1) == c
            t0 = jnp.where(good & same, start, -2048)
            t1 = jnp.where(good & jnp.logical_not(same), start, -2048)
            merge[zz, 0, pl.ds(j * SR, SR), :] = (gap_m == t0).astype(F32).astype(BF16)
            merge[zz, 1, pl.ds(j * SR, SR), :] = (gap_m == t1).astype(F32).astype(BF16)
        return carry

    lax.fori_loop(0, 16, pick_step, 0)
    loads[0].wait()
    transpose_some(0, 6)
    slab.issue(1)

    def swap_copy():
        return remote(w.at[rows_of(f), :], w2.at[rows_of(4 * h + f % 4), :], pe_s, pe_r, swapped)

    @pl.when(moves)
    def _():
        swap_copy().start()

    slab.forward(0)
    lax.fori_loop(16, 32, pick_step, 0)
    lax.fori_loop(0, 4, merge_step, 0)
    transpose_some(6, 12)
    slab.issue(2)
    slab.last(0)
    slab.forward(1)

    transpose_some(12, 20)
    slab.issue(3)
    loads[1].wait()
    loads[2].wait()
    for q in range(4):
        part = pl.ds(q * QS, QR)
        st[q, 0] = param[part, :].astype(BF16)
        st[q, 1] = first[part, :].astype(BF16)
        st[q, 2] = second[part, :].astype(BF16)

    @pl.when(moves)
    def _():
        swap_copy().wait_recv()

    rows2.lines()
    slab.last(1)
    slab.forward(2)
    transpose_some(20, 29)
    slab.last(2)

    slab.forward(3)
    rows2.issue(0)


    def add_pre(k):
        part = pl.ds(pl.multiple_of(zk[k] * 8 * RB, 128), 8 * RB)
        term = jnp.dot(tok[:, part], w[part, :], preferred_element_type=F32)
        if k:
            acc[pl.ds(0, TOK), :] += term
        else:
            acc[pl.ds(0, TOK), :] = term

    for k in range(2):
        slab.wait_core(k)
        add_pre(k)
    slab.last(3)

    rows2.issue(1)

    xcopies = {}
    for i, to in enumerate(xs):
        row = 4 * (4 * hi + (x + 1 + i) % 4) + c
        for b in range(2):
            xcopies[i, b] = send(
                w.at[rows_of(row + 2 * b), :], w2.at[rows_of(4 * h + 2 * b + c), :],
                xc_s.at[2 * i + b], xc_r.at[2 * i + b], to,
            )
    for k in range(2, 4):
        slab.wait_core(k)
    span = pl.ds(pl.multiple_of(h * IG, 16), IG)
    own_rows = pltpu.make_async_copy(w.at[span, :], w2.at[span, :], in_sem.at[3])
    own_rows.start()

    for k in (2, 3):
        add_pre(k)
    pre = acc[pl.ds(0, TOK), :]
    dz_own[...] = (out_grad[...].astype(F32) * gelu_slope(pre)).astype(BF16)

    slab.finish()

    @pl.when(moves)
    def _():
        swap_copy().wait_send()

    swap = []
    for s, k in enumerate((3, 2, 1, 0)):
        def partner_block(j, carry, k=k, s=s):
            w[rows_of(16 * (1 - hi) + s * 4 + j), :] = jnp.dot(
                tokT[rows_of(idx(zx[k], j, 1 - c)), :], dz_own[...], preferred_element_type=F32
            ).astype(BF16)
            return carry

        lax.fori_loop(0, 4, partner_block, 0)
        area = pl.ds(s * 4 * RB, 4 * RB)
        part = pl.ds(pl.multiple_of((16 * (1 - hi) + s * 4) * RB, 16), 4 * RB)
        swap.append(send(w.at[part, :], rxp.at[area, :], rs_s.at[s], rs_r.at[s], partner))
    states.start()
    dz_far = send(dz_own, dz_all.at[h], dz_s.at[0], dz_r.at[0], opposite)
    dz_all[h] = dz_own[...]

    def chip_block(k, s, yy):
        mine = jnp.dot(tokT[rows_of(idx(zx[k], yy, c)), :], dz_own[...], preferred_element_type=F32)
        return mine + rxp[rows_of(s * 4 + yy), :].astype(F32)

    hsend = []

    def half(s, k):
        swap[s].wait_recv()
        sendh[s] = chip_block(k, s, yo).astype(BF16)
        one = send(sendh.at[s, pl.ds(0, HA)], rxh.at[s, pl.ds(0, HA)], rs_s.at[4 + s], rs_r.at[4 + s], right)
        two = send(
            sendh.at[s, pl.ds(HA, RB - HA)], rxh.at[s, pl.ds(HA, RB - HA)], rs_s.at[8 + s], rs_r.at[8 + s], left
        )
        hsend.append((one, two))

    fsend = []
    zout = []

    def full(s, k):
        mine = chip_block(k, s, yr)
        hsend[s][0].wait_recv()
        sendf[s, 0, pl.ds(0, HA)] = (mine[:HA] + rxh[s, pl.ds(0, HA)].astype(F32)).astype(BF16)
        sendf[s, 0, pl.ds(HA, RB - HA)] = mine[HA:].astype(BF16)
        one = send(sendf.at[s, 0], rxf.at[s, 0], rs_s.at[12 + s], rs_r.at[12 + s], right)
        mine = chip_block(k, s, yl)
        hsend[s][1].wait_recv()
        sendf[s, 1, pl.ds(0, HA)] = mine[:HA].astype(BF16)
        sendf[s, 1, pl.ds(HA, RB - HA)] = (mine[HA:] + rxh[s, pl.ds(HA, RB - HA)].astype(F32)).astype(BF16)
        two = send(sendf.at[s, 1], rxf.at[s, 1], rs_s.at[16 + s], rs_r.at[16 + s], left)
        fsend.append((one, two))

    def ring_sum(s, k):
        mine = chip_block(k, s, y)
        fsend[s][0].wait_recv()
        fsend[s][1].wait_recv()
        return mine + rxf[s, 0].astype(F32) + rxf[s, 1].astype(F32)

    def line(s, k):
        sendz[s] = ring_sum(s, k).astype(BF16)
        zout.append(send(sendz.at[s], rxz.at[s], rs_s.at[20 + s], rs_r.at[20 + s], line_to[k]))

    half(0, 3)
    half(1, 2)
    full(0, 3)
    half(2, 1)
    dz_far.wait_recv()
    dz_x = []
    for i, to in enumerate(xs):
        dz_x.append(send(dz_own, dz_all.at[h], dz_s.at[1 + i], dz_r.at[1 + i], to))
        other = (1 - hi) * 4 + x
        dz_x.append(send(dz_all.at[other], dz_all.at[other], dz_s.at[4 + i], dz_r.at[4 + i], to))
    full(1, 2)
    line(0, 3)
    half(3, 0)
    full(2, 1)
    line(1, 2)
    states.far()
    full(3, 0)
    line(2, 1)
    total = ring_sum(3, 0)
    for s in range(3):
        zout[s].wait_recv()
        total = total + rxz[s].astype(F32)

    grad[...] = total * (1.0 / 90.50966799187809)
    for q in range(4):
        gp[q] = grad[pl.ds(q * QS, QR), :].astype(BF16)
    grads.start()
    updated, moment, spread = adam_step(param[...], first[...], second[...], grad[...])
    new_state[0] = updated
    new_state[1] = moment
    new_state[2] = spread
    p16[...] = updated.astype(BF16)

    ysend, csend, msend, xcore = {}, {}, {}, {}

    def offer_to(k):
        zz = zx[k]

        def offer_step(yy, carry):
            sel = pick[pl.ds(yy * 8 + zz * 2, 2)].reshape(2 * PR, RB)
            offer[yy, zz] = jnp.dot(sel, p16[...], preferred_element_type=F32).astype(BF16)
            return carry

        lax.fori_loop(0, 4, offer_step, 0)

    def offer_send(k):
        zz = zx[k]
        for i, (yy, to) in enumerate(((yo, across), (yr, right), (yl, left))):
            ysend[k, i] = send(offer.at[yy, zz], taken.at[y, zz], wr_s.at[k * 4 + i], wr_r.at[k * 4 + i], to)
        taken[y, zz] = offer[y, zz]

    def to_core(k):
        for i in range(3):
            ysend[k, i].wait_recv()
        src = taken.at[:, zx[k], pl.ds(pl.multiple_of((1 - c) * PR, PR), PR), :]
        csend[k] = send(src, taken2.at[zx[k]], wr_s.at[k * 4 + 3], wr_r.at[k * 4 + 3], partner)

    def merge_to(k):
        csend[k].wait_recv()
        zz = zx[k]
        mine = taken[:, zz, pl.ds(pl.multiple_of(c * PR, PR), PR), :].reshape(4 * PR, CB)
        other = taken2[zz].reshape(4 * PR, CB)
        both = jnp.dot(merge[zz, 0], mine, preferred_element_type=F32) + jnp.dot(
            merge[zz, 1], other, preferred_element_type=F32
        )
        merged[k] = both.astype(BF16)
        if k:
            msend[k] = send(merged.at[k], rxm.at[k], wr_s.at[16 + k], wr_r.at[16 + k], line_to[k])

    def x_to_core(i):
        for b in range(2):
            xcopies[i, b].wait_recv()
            slot = rows_of(4 * (4 * hi + (x + 3 - i) % 4) + 2 * b + c)
            xcore[i, b] = send(w2.at[slot, :], w2.at[slot, :], xc_s.at[6 + 2 * i + b], xc_r.at[6 + 2 * i + b], partner)

    offer_to(3)
    offer_send(3)
    offer_to(2)
    offer_send(2)
    offer_to(1)
    offer_to(0)
    rows2.forward(0)
    to_core(3)
    offer_send(1)
    to_core(2)
    offer_send(0)
    rows2.forward(1)
    merge_to(3)
    merge_to(2)
    states.end()
    grads.far()
    for i in range(3):
        x_to_core(i)
    to_core(1)
    to_core(0)
    merge_to(1)
    merge_to(0)

    rows2.last(0)
    grads.end()
    for copy in dz_x:
        copy.wait_recv()
    own_rows.wait()

    def add_term(hh, first_one=False):
        term = dot_t(w2[pl.ds(pl.multiple_of(hh * IG, 16), IG), :], dz_all[hh])
        if first_one:
            acc[...] = term
        else:
            acc[...] += term

    add_term(h, True)
    rows2.last(1)
    for i in range(3):
        for b in range(2):
            xcore[i, b].wait_recv()
        add_term(4 * hi + (x + 3 - i) % 4)
    states.arrived()
    grads.arrived()
    for q in range(4):
        n = QR if q == 3 else QS
        u, m, v = adam_step(
            nst[q, 0, :n].astype(F32), nst[q, 1, :n].astype(F32), nst[q, 2, :n].astype(F32), ngp[q, :n].astype(F32)
        )
        backup[0, pl.ds(q * QS, n)] = u
        backup[1, pl.ds(q * QS, n)] = m
        backup[2, pl.ds(q * QS, n)] = v
    for k in range(2):
        rows2.wait_core(k)
        for half_ in range(2):
            add_term(2 * order2[k] + half_)
    input_grad[...] = acc[...].astype(BF16)
    for k in (1, 2, 3):
        msend[k].wait_recv()
    for j in range(8):
        rows = pl.ds(j * SR, SR)
        piece = (merged[0, rows].astype(F32) + rxm[1, rows].astype(F32)) + (
            rxm[2, rows].astype(F32) + rxm[3, rows].astype(F32)
        )
        written[0, 0, :, j, :] = piece[:PC]
    states.finish()
    grads.finish()
    rows2.finish()
    for copy in pending:
        copy.wait_send()


def kernel_call(*args):
    vmem = pl.BlockSpec(memory_space=pltpu.VMEM)
    hbm = pl.BlockSpec(memory_space=pl.ANY)
    dma = pltpu.SemaphoreType.DMA
    V = pltpu.VMEM
    return pl.pallas_call(
        kernel,
        name="slab",
        out_shape=(
            pltpu.VMEM((IG, TOK), BF16),
            pltpu.VMEM((3, RB, CB), F32),
            pltpu.VMEM((3, RB, CB), F32),
            pltpu.VMEM((1, 1, PC, 8, CB), F32),
        ),
        in_specs=[hbm, vmem, vmem, hbm, hbm, pl.BlockSpec(memory_space=pltpu.SMEM)],
        out_specs=(vmem,) * 4,
        scratch_shapes=[
            V((TOK, DM), BF16), V((DM, TOK), BF16), V((DM, CB), BF16), V((DM, CB), BF16),
            V((16 * RB, CB), BF16), V((4, RB, CB), BF16), V((4, RB, CB), BF16),
            V((4, 2, RB, CB), BF16), V((4, 2, RB, CB), BF16), V((3, RB, CB), BF16), V((3, RB, CB), BF16),
            V((TOK, CB), BF16), V((8, TOK, CB), BF16),
            V((RB, CB), F32), V((RB, CB), F32),
            V((4, 3, QR, CB), BF16), V((4, 3, QR, CB), BF16), V((3, QR, CB), BF16), V((3, QR, CB), BF16),
            V((4, QR, CB), BF16), V((4, QR, CB), BF16), V((QR, CB), BF16), V((QR, CB), BF16),
            V((IG, TOK), F32), V((RB, CB), F32), V((RB, CB), BF16),
            V((32, PR, RB), BF16), V((4, 2, 8 * SR, 4 * PR), BF16),
            V((4, 4, 2 * PR, CB), BF16), V((4, 4, 2 * PR, CB), BF16), V((4, 4, PR, CB), BF16),
            V((4, 8 * SR, CB), BF16), V((4, 8 * SR, CB), BF16),
            dma((12,)), dma((12,)), dma((8,)), dma((38,)), dma((38,)), dma((38,)), dma((38,)), dma((24,)), dma((24,)),
            dma((7,)), dma((7,)), dma, dma, dma((16,)), dma((16,)), dma((20,)), dma((20,)),
        ],
        compiler_params=pltpu.CompilerParams(
            collective_id=0, has_side_effects=True, vmem_limit_bytes=58 * 1024 * 1024
        ),
        cost_estimate=pl.CostEstimate(
            flops=6 * TOK * DM * CB, bytes_accessed=20_000_000, transcendentals=2 * TOK * CB
        ),
    )(*args)


def on_device(tokens, out_grad, param, first, second, sources):
    input_grad, new_state, backup, written = kernel_call(
        tokens, out_grad, param, first, second, sources.transpose(0, 2, 1)
    )
    return (input_grad.T, new_state, backup, written.transpose(0, 1, 3, 2, 4))


def solution(mesh):
    return jax.shard_map(
        on_device,
        mesh=mesh,
        in_specs=(
            P("fsdp", None),
            P("fsdp", "hst"),
            P("fsdp", "hst"),
            P("fsdp", "hst"),
            P("fsdp", "hst"),
            P("hst", None, None),
        ),
        out_specs=(
            P("fsdp", "hst"),
            P(None, "fsdp", "hst"),
            P(None, "fsdp", "hst"),
            P("hst", "fsdp", None, None, None),
        ),
        check_vma=False,
    )
```

```python
import functools

import jax
import jax.numpy as jnp
from jax import lax
from jax.experimental import pallas as pl
from jax.experimental.pallas import tpu as pltpu
from jax.sharding import PartitionSpec as P

MESH = pl.DeviceIdType.MESH
BF16 = jnp.bfloat16
F32 = jnp.float32
I32 = jnp.int32
TOK = 256
RB = 464
CB = 256
DM = 32 * RB
IG = DM // 8
HA = 240
PC = 29
PR = 64
SR = 32
QS, QR = 112, 128


def gelu_slope(pre):
    cdf = 0.5 * (1.0 + lax.erf(pre * 0.7071067811865476))
    pdf = jnp.exp(-0.5 * pre * pre) * 0.3989422804014327
    return cdf + pre * pdf


def adam_step(param, first, second, grad):
    moment = 0.8 * first + 0.2 * grad
    spread = 0.9 * second + 0.1 * grad * grad
    updated = param - 0.1 * (moment / (jnp.sqrt(spread) + 1e-08) + 0.1 * param)
    return (updated, moment, spread)


def rows_of(f):
    return pl.ds(pl.multiple_of(f * RB, 16), RB)


def dot_t(a, b):
    return lax.dot_general(a, b, (((1,), (1,)), ((), ())), preferred_element_type=F32)


def kernel(
    tokens, out_grad, param, first_in, second_in, sources,
    input_grad, new_state, backup, written,
    tok, tokT, w, w2, rxp, sendh, rxh, sendf, rxf, sendz, rxz, dz_own, dz_all,
    first, second, st, nst, st1, st2, gp, ngp, gp1, gp2, acc, grad, p16,
    pick, merge, offer, taken, taken2, merged, rxm,
    xc_s, xc_r, in_sem, ag_s, ag_r, bg_s, bg_r, rs_s, rs_r, dz_s, dz_r, pe_s, pe_r, re_s, re_r, wr_s, wr_r,
):
    f = lax.axis_index("fsdp")
    h = lax.axis_index("hst")
    z, y, c = f // 8, (f // 2) % 4, f % 2
    hi, x = h // 4, h % 4
    yr, yl, yo = (y + 1) % 4, (y + 3) % 4, (y + 2) % 4
    near = z + 1 - 2 * (z % 2)
    zx = [z, near, (z + 2) % 4, 3 - z]
    zk = [z, near, 2 - z // 2, 3 - 3 * (z // 2)]
    inner = (z == 1) | (z == 2)

    def idx(zz, yy, cc):
        return zz * 8 + yy * 2 + cc

    def at(zz, yy, cc):
        return {"fsdp": idx(zz, yy, cc)}

    def over(ww, xx):
        return {"hst": ww * 4 + xx}

    right, left, partner, across = at(z, yr, c), at(z, yl, c), at(z, y, 1 - c), at(z, yo, c)
    line_to = [None] + [at(zx[k], y, c) for k in (1, 2, 3)]
    opposite = over(1 - hi, x)
    xs = [over(hi, (x + i) % 4) for i in (1, 2, 3)]
    swapped = {"fsdp": 4 * h + f % 4, "hst": f // 4}
    member = (z // 2 + hi) % 2
    moves = member == 1
    stays = member == 0
    order2 = [member * z + (1 - member) * (2 - hi), member * near + (1 - member) * (3 - 3 * hi)]

    loads = [
        pltpu.make_async_copy(a, b, in_sem.at[i])
        for i, (a, b) in enumerate(((tokens, tok), (first_in, first), (second_in, second)))
    ]
    for load in loads:
        load.start()

    barrier = pltpu.get_barrier_semaphore()
    for peer in (right, left, across, partner, *line_to[1:], opposite, *xs):
        pl.semaphore_signal(barrier, inc=1, device_id=peer, device_id_type=MESH)

    @pl.when(moves)
    def _():
        pl.semaphore_signal(barrier, inc=1, device_id=swapped, device_id_type=MESH)

    w[rows_of(f), :] = param[...].astype(BF16)

    @pl.when(moves)
    def _():
        pl.semaphore_wait(barrier, 12)

    @pl.when(stays)
    def _():
        pl.semaphore_wait(barrier, 11)

    pending = []

    def remote(src, dst, s_sem, r_sem, to):
        return pltpu.make_async_remote_copy(
            src_ref=src, dst_ref=dst, send_sem=s_sem, recv_sem=r_sem, device_id=to, device_id_type=MESH
        )

    def send(src, dst, s_sem, r_sem, to):
        copy = remote(src, dst, s_sem, r_sem, to)
        copy.start()
        pending.append(copy)
        return copy

    class Gather:
        def __init__(self, buf, s_sem, r_sem, order):
            self.buf, self.s, self.r, self.zk = buf, s_sem, r_sem, order
            self.own, self.core, self.halves = {}, {}, {}
            self.sent, self.some, self.came = [], [], set()

        def copy(self, block, lo, n, s_sem, r_sem, to):
            ref = self.buf.at[pl.ds(pl.multiple_of(block * RB + lo, 16), n), :]
            return remote(ref, ref, self.s.at[s_sem], self.r.at[r_sem], to)

        def put(self, block, lo, n, sem, to):
            copy = self.copy(block, lo, n, sem, sem, to)
            copy.start()
            self.sent.append(copy)
            return copy

        def put_some(self, cond, block, s_sem, r_sem, to):
            copy = self.copy(block, 0, RB, s_sem, r_sem, to)
            pl.when(cond)(copy.start)
            self.some.append((cond, copy))

        def lines(self):
            self.put_some(z >= 0, f, 33, 33, line_to[1])
            self.put_some(inner, f, 34, 34, line_to[3])

        def arrive(self, k):
            self.came.add(k)
            if k == 0:
                return
            b = idx(self.zk[k], y, c)
            self.copy(b, 0, RB, 33, 32 + k, line_to[1]).wait_recv()
            self.put_some(inner, b, 34 + k, (35, 34, 35)[k - 1], (line_to[3], line_to[1], line_to[1])[k - 1])

        def issue(self, k):
            self.arrive(k)
            b = idx(self.zk[k], y, c)
            self.own[k] = (self.put(b, 0, RB, k * 8, right), self.put(b, 0, RB, k * 8 + 1, left))
            self.core[k, 0] = self.put(b, 0, RB, k * 8 + 4, partner)

        def forward(self, k):
            self.own[k][0].wait_recv()
            b = idx(self.zk[k], yl, c)
            one = self.put(b, 0, HA, k * 8 + 2, right)
            self.core[k, 1] = self.put(b, 0, RB, k * 8 + 5, partner)
            self.own[k][1].wait_recv()
            b = idx(self.zk[k], yr, c)
            two = self.put(b, HA, RB - HA, k * 8 + 3, left)
            self.core[k, 2] = self.put(b, 0, RB, k * 8 + 6, partner)
            self.halves[k] = (one, two)

        def last(self, k):
            self.halves[k][0].wait_recv()
            self.halves[k][1].wait_recv()
            self.core[k, 3] = self.put(idx(self.zk[k], yo, c), 0, RB, k * 8 + 7, partner)

        def wait_core(self, k):
            for j in range(4):
                self.core[k, j].wait_recv()

        def finish(self):
            for copy in self.sent:
                copy.wait_send()
            for cond, copy in self.some:
                pl.when(cond)(copy.wait_send)

    class HalfGather(Gather):
        def lines(self):
            self.put_some(moves, f, 33, 34, line_to[1])
            self.put_some(moves & inner, f, 34, 33, line_to[3])

        def arrive(self, k):
            self.came.add(k)
            b = idx(self.zk[k], y, c)
            came = self.copy(b, 0, RB, 33, 33 + k, line_to[1])
            if k == 0:
                pl.when(stays)(came.wait_recv)
                self.put_some(stays & inner, b, 35, 33, line_to[1])
            else:
                came.wait_recv()
                self.put_some(moves & inner, b, 36, 34, line_to[3])
                self.put_some(stays & inner, b, 37, 34, line_to[1])

    def transpose_some(lo, hi_):
        def step(i, carry):
            cols = pl.ds(pl.multiple_of(i * 512, 512), 512)
            tokT[cols, :] = tok[:, cols].T
            return carry

        lax.fori_loop(lo, hi_, step, 0)

    class Relay:
        def __init__(self, src, dst, one, two, sem):
            self.src, self.dst, self.one, self.two = src, dst, one, two
            self.s = [re_s.at[sem + i] for i in range(7)]
            self.r = [re_r.at[sem + i] for i in range(7)]

        def to_next(self):
            return remote(self.src, self.dst, self.s[0], self.r[0], over(hi, (x + 1) % 4))

        def to_column(self, q):
            return remote(self.src.at[q], self.one, self.s[1 + q], self.r[1], over(hi, q))

        def to_far(self, src):
            return remote(src, self.two, self.s[4], self.r[4], opposite)

        def start(self):
            @pl.when(x < 3)
            def _():
                self.to_next().start()

            @pl.when(x == 3)
            def _():
                for q in range(3):
                    self.to_column(q).start()
                self.to_far(self.src.at[3]).start()

        def far(self):
            @pl.when(x < 3)
            def _():
                self.to_column(0).wait_recv()
                self.to_far(self.one).start()

        def end(self):
            self.to_far(self.one).wait_recv()

            @pl.when(x == 0)
            def _():
                self.dst[0] = self.two[...]

            for q in (1, 2, 3):
                @pl.when(x == q)
                def _(q=q):
                    remote(self.two, self.dst.at[q], self.s[5], self.end_sem(q), over(hi, 0)).start()

        def end_sem(self, q):
            return (self.r[5], self.r[6], self.r[2])[q - 1]

        def arrived(self):
            @pl.when(x > 0)
            def _():
                self.to_next().wait_recv()

            @pl.when(x == 0)
            def _():
                for q in (1, 2, 3):
                    remote(self.two, self.dst.at[q], self.s[5], self.end_sem(q), over(hi, 1)).wait_recv()

        def finish(self):
            @pl.when(x < 3)
            def _():
                self.to_next().wait_send()
                self.to_far(self.one).wait_send()

            @pl.when(x == 3)
            def _():
                for q in range(3):
                    self.to_column(q).wait_send()
                self.to_far(self.src.at[3]).wait_send()

            @pl.when(x > 0)
            def _():
                remote(self.two, self.dst.at[1], self.s[5], self.r[5], over(hi, 0)).wait_send()

    slab = Gather(w, ag_s, ag_r, zk)
    rows2 = HalfGather(w2, bg_s, bg_r, order2)
    states = Relay(st, nst, st1, st2, 0)
    grads = Relay(gp, ngp, gp1, gp2, 8)

    slab.lines()
    slab.issue(0)

    row_p = lax.broadcasted_iota(I32, (PR, RB), 0)
    col_p = lax.broadcasted_iota(I32, (PR, RB), 1)
    gap0 = jnp.where(row_p < PC, col_p - row_p, -4096)
    gap1 = jnp.where((row_p >= PC) & (row_p < 2 * PC), col_p - row_p + PC, -4096)

    def pick_step(n, carry):
        writer = ((n // 2) % 4) * 8 + (n // 8) * 2 + n % 2
        a = jnp.int32(-1)
        b = jnp.int32(-1)
        for j in range(8):
            s = sources[0, j, writer]
            here = (s >= 0) & (lax.shift_right_arithmetic(s, 4) == f)
            piece = jnp.bitwise_and(s, 15)
            b = jnp.where(here & (a >= 0), piece, b)
            a = jnp.where(here & (a < 0), piece, a)
        pick[n] = ((gap0 == a * PC) | (gap1 == b * PC)).astype(F32).astype(BF16)
        return carry

    row_m = lax.broadcasted_iota(I32, (SR, 4 * PR), 0)
    col_m = lax.broadcasted_iota(I32, (SR, 4 * PR), 1)
    gap_m = jnp.where(row_m < PC, col_m - row_m, -4096)

    def merge_step(zz, carry):
        writer = idx(zz, y, c)
        entry = [sources[0, j, writer] for j in range(8)]
        owner = [lax.shift_right_arithmetic(s, 4) for s in entry]
        for j in range(8):
            rank = jnp.int32(0)
            for i in range(j):
                rank = rank + jnp.where(owner[i] == owner[j], 1, 0)
            good = (entry[j] >= 0) & (lax.shift_right_arithmetic(owner[j], 3) == z)
            start = jnp.bitwise_and(lax.shift_right_arithmetic(owner[j], 1), 3) * PR + rank * PC
            same = jnp.bitwise_and(owner[j], 1) == c
            t0 = jnp.where(good & same, start, -2048)
            t1 = jnp.where(good & jnp.logical_not(same), start, -2048)
            merge[zz, 0, pl.ds(j * SR, SR), :] = (gap_m == t0).astype(F32).astype(BF16)
            merge[zz, 1, pl.ds(j * SR, SR), :] = (gap_m == t1).astype(F32).astype(BF16)
        return carry

    lax.fori_loop(0, 16, pick_step, 0)
    loads[0].wait()
    transpose_some(0, 6)
    slab.issue(1)

    def swap_copy():
        return remote(w.at[rows_of(f), :], w2.at[rows_of(4 * h + f % 4), :], pe_s, pe_r, swapped)

    @pl.when(moves)
    def _():
        swap_copy().start()

    slab.forward(0)
    lax.fori_loop(16, 32, pick_step, 0)
    lax.fori_loop(0, 4, merge_step, 0)
    transpose_some(6, 12)
    slab.issue(2)
    slab.last(0)
    slab.forward(1)

    transpose_some(12, 20)
    slab.issue(3)
    loads[1].wait()
    loads[2].wait()
    for q in range(4):
        part = pl.ds(q * QS, QR)
        st[q, 0] = param[part, :].astype(BF16)
        st[q, 1] = first[part, :].astype(BF16)
        st[q, 2] = second[part, :].astype(BF16)

    @pl.when(moves)
    def _():
        swap_copy().wait_recv()

    rows2.lines()
    slab.last(1)
    slab.forward(2)
    transpose_some(20, 29)
    slab.last(2)

    slab.forward(3)


    def add_pre(k):
        part = pl.ds(pl.multiple_of(zk[k] * 8 * RB, 128), 8 * RB)
        term = jnp.dot(tok[:, part], w[part, :], preferred_element_type=F32)
        if k:
            acc[pl.ds(0, TOK), :] += term
        else:
            acc[pl.ds(0, TOK), :] = term

    for k in range(2):
        slab.wait_core(k)
        add_pre(k)
    rows2.issue(0)
    rows2.issue(1)
    slab.last(3)


    for k in range(2, 4):
        slab.wait_core(k)
    span = pl.ds(pl.multiple_of(h * IG, 16), IG)
    own_rows = pltpu.make_async_copy(w.at[span, :], w2.at[span, :], in_sem.at[3])
    own_rows.start()

    for k in (2, 3):
        add_pre(k)
    pre = acc[pl.ds(0, TOK), :]
    dz_own[...] = (out_grad[...].astype(F32) * gelu_slope(pre)).astype(BF16)

    slab.finish()

    @pl.when(moves)
    def _():
        swap_copy().wait_send()

    swap = []
    for s, k in enumerate((3, 2, 1, 0)):
        def partner_block(j, carry, k=k, s=s):
            w[rows_of(16 * (1 - hi) + s * 4 + j), :] = jnp.dot(
                tokT[rows_of(idx(zx[k], j, 1 - c)), :], dz_own[...], preferred_element_type=F32
            ).astype(BF16)
            return carry

        lax.fori_loop(0, 4, partner_block, 0)
        area = pl.ds(s * 4 * RB, 4 * RB)
        part = pl.ds(pl.multiple_of((16 * (1 - hi) + s * 4) * RB, 16), 4 * RB)
        swap.append(send(w.at[part, :], rxp.at[area, :], rs_s.at[s], rs_r.at[s], partner))
    dz_far = send(dz_own, dz_all.at[h], dz_s.at[0], dz_r.at[0], opposite)
    dz_all[h] = dz_own[...]
    states.start()
    xcopies = {}
    for i, to in enumerate(xs):
        row = 4 * (4 * hi + (x + 1 + i) % 4) + c
        for b in range(2):
            xcopies[i, b] = send(
                w.at[rows_of(row + 2 * b), :], w2.at[rows_of(4 * h + 2 * b + c), :],
                xc_s.at[2 * i + b], xc_r.at[2 * i + b], to,
            )

    def chip_block(k, s, yy):
        mine = jnp.dot(tokT[rows_of(idx(zx[k], yy, c)), :], dz_own[...], preferred_element_type=F32)
        return mine + rxp[rows_of(s * 4 + yy), :].astype(F32)

    hsend = []

    def half(s, k):
        swap[s].wait_recv()
        sendh[s] = chip_block(k, s, yo).astype(BF16)
        one = send(sendh.at[s, pl.ds(0, HA)], rxh.at[s, pl.ds(0, HA)], rs_s.at[4 + s], rs_r.at[4 + s], right)
        two = send(
            sendh.at[s, pl.ds(HA, RB - HA)], rxh.at[s, pl.ds(HA, RB - HA)], rs_s.at[8 + s], rs_r.at[8 + s], left
        )
        hsend.append((one, two))

    fsend = []
    zout = []

    def full(s, k):
        mine = chip_block(k, s, yr)
        hsend[s][0].wait_recv()
        sendf[s, 0, pl.ds(0, HA)] = (mine[:HA] + rxh[s, pl.ds(0, HA)].astype(F32)).astype(BF16)
        sendf[s, 0, pl.ds(HA, RB - HA)] = mine[HA:].astype(BF16)
        one = send(sendf.at[s, 0], rxf.at[s, 0], rs_s.at[12 + s], rs_r.at[12 + s], right)
        mine = chip_block(k, s, yl)
        hsend[s][1].wait_recv()
        sendf[s, 1, pl.ds(0, HA)] = mine[:HA].astype(BF16)
        sendf[s, 1, pl.ds(HA, RB - HA)] = (mine[HA:] + rxh[s, pl.ds(HA, RB - HA)].astype(F32)).astype(BF16)
        two = send(sendf.at[s, 1], rxf.at[s, 1], rs_s.at[16 + s], rs_r.at[16 + s], left)
        fsend.append((one, two))

    def ring_sum(s, k):
        mine = chip_block(k, s, y)
        fsend[s][0].wait_recv()
        fsend[s][1].wait_recv()
        return mine + rxf[s, 0].astype(F32) + rxf[s, 1].astype(F32)

    def line(s, k):
        sendz[s] = ring_sum(s, k).astype(BF16)
        zout.append(send(sendz.at[s], rxz.at[s], rs_s.at[20 + s], rs_r.at[20 + s], line_to[k]))

    half(0, 3)
    half(1, 2)
    full(0, 3)
    half(2, 1)
    dz_far.wait_recv()
    dz_x = []
    for i, to in enumerate(xs):
        dz_x.append(send(dz_own, dz_all.at[h], dz_s.at[1 + i], dz_r.at[1 + i], to))
        other = (1 - hi) * 4 + x
        dz_x.append(send(dz_all.at[other], dz_all.at[other], dz_s.at[4 + i], dz_r.at[4 + i], to))
    full(1, 2)
    line(0, 3)
    half(3, 0)
    full(2, 1)
    line(1, 2)
    states.far()
    full(3, 0)
    line(2, 1)
    total = ring_sum(3, 0)
    for s in range(3):
        zout[s].wait_recv()
        total = total + rxz[s].astype(F32)

    grad[...] = total * (1.0 / 90.50966799187809)
    for q in range(4):
        gp[q] = grad[pl.ds(q * QS, QR), :].astype(BF16)
    grads.start()
    updated, moment, spread = adam_step(param[...], first[...], second[...], grad[...])
    new_state[0] = updated
    new_state[1] = moment
    new_state[2] = spread
    p16[...] = updated.astype(BF16)

    ysend, csend, msend, xcore = {}, {}, {}, {}

    def offer_to(k):
        zz = zx[k]

        def offer_step(yy, carry):
            sel = pick[pl.ds(yy * 8 + zz * 2, 2)].reshape(2 * PR, RB)
            offer[yy, zz] = jnp.dot(sel, p16[...], preferred_element_type=F32).astype(BF16)
            return carry

        lax.fori_loop(0, 4, offer_step, 0)

    def offer_send(k):
        zz = zx[k]
        for i, (yy, to) in enumerate(((yo, across), (yr, right), (yl, left))):
            ysend[k, i] = send(offer.at[yy, zz], taken.at[y, zz], wr_s.at[k * 4 + i], wr_r.at[k * 4 + i], to)
        taken[y, zz] = offer[y, zz]

    def to_core(k):
        for i in range(3):
            ysend[k, i].wait_recv()
        src = taken.at[:, zx[k], pl.ds(pl.multiple_of((1 - c) * PR, PR), PR), :]
        csend[k] = send(src, taken2.at[zx[k]], wr_s.at[k * 4 + 3], wr_r.at[k * 4 + 3], partner)

    def merge_to(k):
        csend[k].wait_recv()
        zz = zx[k]
        mine = taken[:, zz, pl.ds(pl.multiple_of(c * PR, PR), PR), :].reshape(4 * PR, CB)
        other = taken2[zz].reshape(4 * PR, CB)
        both = jnp.dot(merge[zz, 0], mine, preferred_element_type=F32) + jnp.dot(
            merge[zz, 1], other, preferred_element_type=F32
        )
        merged[k] = both.astype(BF16)
        if k:
            msend[k] = send(merged.at[k], rxm.at[k], wr_s.at[16 + k], wr_r.at[16 + k], line_to[k])

    def x_to_core(i):
        for b in range(2):
            xcopies[i, b].wait_recv()
            slot = rows_of(4 * (4 * hi + (x + 3 - i) % 4) + 2 * b + c)
            xcore[i, b] = send(w2.at[slot, :], w2.at[slot, :], xc_s.at[6 + 2 * i + b], xc_r.at[6 + 2 * i + b], partner)

    offer_to(3)
    offer_send(3)
    offer_to(2)
    offer_send(2)
    offer_to(1)
    offer_to(0)
    rows2.forward(0)
    to_core(3)
    offer_send(1)
    to_core(2)
    offer_send(0)
    rows2.forward(1)
    merge_to(3)
    merge_to(2)
    states.end()
    grads.far()
    for i in range(3):
        x_to_core(i)
    to_core(1)
    to_core(0)
    merge_to(1)
    merge_to(0)

    rows2.last(0)
    grads.end()
    for copy in dz_x:
        copy.wait_recv()
    own_rows.wait()

    def add_term(hh, first_one=False):
        term = dot_t(w2[pl.ds(pl.multiple_of(hh * IG, 16), IG), :], dz_all[hh])
        if first_one:
            acc[...] = term
        else:
            acc[...] += term

    add_term(h, True)
    rows2.last(1)
    for i in range(3):
        for b in range(2):
            xcore[i, b].wait_recv()
        add_term(4 * hi + (x + 3 - i) % 4)
    states.arrived()
    grads.arrived()
    for q in range(4):
        n = QR if q == 3 else QS
        u, m, v = adam_step(
            nst[q, 0, :n].astype(F32), nst[q, 1, :n].astype(F32), nst[q, 2, :n].astype(F32), ngp[q, :n].astype(F32)
        )
        backup[0, pl.ds(q * QS, n)] = u
        backup[1, pl.ds(q * QS, n)] = m
        backup[2, pl.ds(q * QS, n)] = v
    for k in range(2):
        rows2.wait_core(k)
        for half_ in range(2):
            add_term(2 * order2[k] + half_)
    input_grad[...] = acc[...].astype(BF16)
    for k in (1, 2, 3):
        msend[k].wait_recv()
    for j in range(8):
        rows = pl.ds(j * SR, SR)
        piece = (merged[0, rows].astype(F32) + rxm[1, rows].astype(F32)) + (
            rxm[2, rows].astype(F32) + rxm[3, rows].astype(F32)
        )
        written[0, 0, :, j, :] = piece[:PC]
    states.finish()
    grads.finish()
    rows2.finish()
    for copy in pending:
        copy.wait_send()


def kernel_call(*args):
    vmem = pl.BlockSpec(memory_space=pltpu.VMEM)
    hbm = pl.BlockSpec(memory_space=pl.ANY)
    dma = pltpu.SemaphoreType.DMA
    V = pltpu.VMEM
    return pl.pallas_call(
        kernel,
        name="slab",
        out_shape=(
            pltpu.VMEM((IG, TOK), BF16),
            pltpu.VMEM((3, RB, CB), F32),
            pltpu.VMEM((3, RB, CB), F32),
            pltpu.VMEM((1, 1, PC, 8, CB), F32),
        ),
        in_specs=[hbm, vmem, vmem, hbm, hbm, pl.BlockSpec(memory_space=pltpu.SMEM)],
        out_specs=(vmem,) * 4,
        scratch_shapes=[
            V((TOK, DM), BF16), V((DM, TOK), BF16), V((DM, CB), BF16), V((DM, CB), BF16),
            V((16 * RB, CB), BF16), V((4, RB, CB), BF16), V((4, RB, CB), BF16),
            V((4, 2, RB, CB), BF16), V((4, 2, RB, CB), BF16), V((3, RB, CB), BF16), V((3, RB, CB), BF16),
            V((TOK, CB), BF16), V((8, TOK, CB), BF16),
            V((RB, CB), F32), V((RB, CB), F32),
            V((4, 3, QR, CB), BF16), V((4, 3, QR, CB), BF16), V((3, QR, CB), BF16), V((3, QR, CB), BF16),
            V((4, QR, CB), BF16), V((4, QR, CB), BF16), V((QR, CB), BF16), V((QR, CB), BF16),
            V((IG, TOK), F32), V((RB, CB), F32), V((RB, CB), BF16),
            V((32, PR, RB), BF16), V((4, 2, 8 * SR, 4 * PR), BF16),
            V((4, 4, 2 * PR, CB), BF16), V((4, 4, 2 * PR, CB), BF16), V((4, 4, PR, CB), BF16),
            V((4, 8 * SR, CB), BF16), V((4, 8 * SR, CB), BF16),
            dma((12,)), dma((12,)), dma((8,)), dma((38,)), dma((38,)), dma((38,)), dma((38,)), dma((24,)), dma((24,)),
            dma((7,)), dma((7,)), dma, dma, dma((16,)), dma((16,)), dma((20,)), dma((20,)),
        ],
        compiler_params=pltpu.CompilerParams(
            collective_id=0, has_side_effects=True, vmem_limit_bytes=58 * 1024 * 1024
        ),
        cost_estimate=pl.CostEstimate(
            flops=6 * TOK * DM * CB, bytes_accessed=20_000_000, transcendentals=2 * TOK * CB
        ),
    )(*args)


def on_device(tokens, out_grad, param, first, second, sources):
    input_grad, new_state, backup, written = kernel_call(
        tokens, out_grad, param, first, second, sources.transpose(0, 2, 1)
    )
    return (input_grad.T, new_state, backup, written.transpose(0, 1, 3, 2, 4))


def solution(mesh):
    return jax.shard_map(
        on_device,
        mesh=mesh,
        in_specs=(
            P("fsdp", None),
            P("fsdp", "hst"),
            P("fsdp", "hst"),
            P("fsdp", "hst"),
            P("fsdp", "hst"),
            P("hst", None, None),
        ),
        out_specs=(
            P("fsdp", "hst"),
            P(None, "fsdp", "hst"),
            P(None, "fsdp", "hst"),
            P("hst", "fsdp", None, None, None),
        ),
        check_vma=False,
    )
```
